256 devices in a mesh: replica: 16 (over z, core), tensor: 16 (over x, y).
Axes of the slice: x: 4, y: 4, z: 8, core: 2. Of those that a mesh axis runs over, the one named last changes fastest.
Arguments:
- hidden_in: bfloat16 [8192, 5120], P('replica'), may hold values from -6 to 6
- norm_gain: float32 [5120], replicated, may hold values from 0.1 to 1.9
- w_query: bfloat16 [5120, 4096], P(None, 'tensor'), may hold values from -0.078125 to 0.078125
- w_keyval: bfloat16 [5120, 4096], P(None, 'tensor'), as said below
- query_gain: float32 [128], replicated, may hold values from 0.1 to 1.9
- key_gain: float32 [128], replicated, may hold values from 0.1 to 1.9
- w_output: bfloat16 [4096, 5120], P('tensor'), may hold values from -0.09375 to 0.09375
- kv_pool: bfloat16 [128, 128, 4096], P('replica', None, 'tensor'), as said below
- prefix_len: int32 [16], replicated, may hold values from 3072 to 6144, as said below
- hit_holder: int32 [16, 48], replicated, may hold values from 0 to 15, as said below
- hit_slot: int32 [16, 48], replicated, may hold values from 0 to 7
- dest_holder: int32 [16, 4], replicated, may hold values from 0 to 15, as said below
- dest_slot: int32 [16, 4], replicated, may hold values from 0 to 7
Outputs:
- attended: bfloat16 [8192, 5120], P('replica', 'tensor')
- pool_after: bfloat16 [128, 128, 4096], P('replica', None, 'tensor')
The draws below stay inside these ranges and needn't reach their ends.
Inputs may be any that keep to these rules, and one draw needn't show every extreme that they name: `prefix_len`: one request has exactly 6144 cached tokens, every request at least half of that. `hit_holder`: among the first ceil(prefix_len / 128) entries of a row, no holder appears more than 3 times; the longest request reaches 3 on every holder. The pairs (dest_holder, dest_slot) are all different. `w_keyval`: copies 2 h and 2 h + 1 of every key-value head are equal. `kv_pool`: copies 2 h and 2 h + 1 of every key-value head are equal.
All inputs are finite; a program needn't handle non-finite values.
Results may differ from the reference program's by a relative error of at most 0.02.
The reference program's roundings to bfloat16 on the way count: a program that leaves them out, or rounds other values in their place, can miss the bound.
Values may be sent and summed in bfloat16 or wider, within the bound.
No kernel may reach another device: no remote copies, remote signals or barrier semaphores. Data moves between devices by JAX's collectives and lax.ppermute only.
A program may use at most 256 MiB of HBM per device.

```python
import jax
import jax.numpy as jnp
from jax import lax

D = 5120
HD = 128
KVH = 8
QH = 32
BLK = 128
CAP = 3
SPAN = 512
POOL = 8
REQS = 16
MAXB = 48
NEWB = 4
N_TENSOR = 16


def dest_ids(key):
    order = jax.random.permutation(jax.random.fold_in(key, 7), REQS * POOL)
    return order[:REQS * NEWB].reshape(REQS, NEWB)


def draw_dest_holder(key, part):
    return (dest_ids(key) // POOL).astype(jnp.int32)


def draw_dest_slot(key, part):
    return (dest_ids(key) % POOL).astype(jnp.int32)


def draw_prefix_len(key, part):
    key = jax.random.fold_in(key, 11)
    longest = MAXB * BLK
    lengths = jax.random.randint(key, (REQS,), longest // 2, longest + 1)
    which = jax.random.randint(jax.random.fold_in(key, 1), (), 0, REQS)
    return jnp.where(jnp.arange(REQS) == which, longest, lengths).astype(jnp.int32)


def draw_hit_holder(key, part):
    key = jax.random.fold_in(key, 12)
    keys = jax.random.split(key, REQS)
    order = jax.vmap(lambda single: jax.random.permutation(single, CAP * REQS))(keys)
    return (order[:, :MAXB] % REQS).astype(jnp.int32)


def draw_w_keyval(key, part):
    key = jax.random.fold_in(key, 14)
    values = jax.random.normal(key, (D, KVH, 2 * HD), jnp.float32) * D ** (-0.5)
    return jnp.repeat(values, 2, axis=1).reshape(D, 2 * KVH * 2 * HD).astype(jnp.bfloat16)


def draw_kv_pool(key, part):
    key = jax.random.fold_in(key, 13)
    shape = (REQS * POOL, BLK, KVH, 2 * HD)
    values = jax.random.normal(key, shape, jnp.float32)
    values = jnp.clip(values, -60.0, 60.0)
    return jnp.repeat(values, 2, axis=2).reshape(REQS * POOL, BLK, 2 * KVH * 2 * HD).astype(jnp.bfloat16)


def set_ends(array, own_key, least, high):
    longest = array.shape.index(max(array.shape))
    spots = []
    for shift in (0, 1):
        where = [jax.random.randint(jax.random.fold_in(own_key, axis), (), 0, length) for axis, length in enumerate(array.shape)]
        where[longest] = (where[longest] + shift) % array.shape[longest]
        spots.append(tuple(where))
    return array.at[spots[0]].set(least).at[spots[1]].set(high)


def shard_levels(stream_key, dims, cuts, least, largest):
    loudness = 1.0
    for dim, shards_of in cuts:
        heights = jax.random.uniform(jax.random.fold_in(jax.random.fold_in(stream_key, 6), dim), (shards_of,), jnp.float32, least / len(cuts), largest / len(cuts))
        loudness = loudness * jnp.repeat(jnp.exp(heights), dims[dim] // shards_of).reshape((-1,) + (1,) * (len(dims) - 1 - dim))
    return loudness


def centred(key, dims, deviation, most, pieces=(), held_as=jnp.bfloat16):
    array = deviation * jax.random.normal(key, dims, jnp.float32)
    if pieces:
        array = array * shard_levels(key, dims, pieces, -0.22, 0.18)
    return jnp.clip(array, -most, most).astype(held_as)


def setup_inputs(seed: int = 0) -> dict:
    splits = jax.random.split(jax.random.key(seed), 14)
    return {
        "hidden_in": centred(splits[0], (REQS * SPAN, D), 1.0, 6.0, ((0, 16),)),
        "norm_gain": jnp.clip(1.0 + 0.18 * jax.random.normal(splits[1], (D,), jnp.float32), 0.1, 1.9),
        "w_query": centred(splits[2], (D, QH * HD), D ** -0.5, 0.078125, ((1, 16),)),
        "w_keyval": draw_w_keyval(jax.random.fold_in(splits[13], 71), 0),
        "query_gain": jnp.clip(1.0 + 0.18 * jax.random.normal(splits[4], (HD,), jnp.float32), 0.1, 1.9),
        "key_gain": jnp.clip(1.0 + 0.18 * jax.random.normal(splits[5], (HD,), jnp.float32), 0.1, 1.9),
        "w_output": centred(splits[6], (QH * HD, D), (QH * HD) ** -0.5, 0.09375, ((0, 16),)),
        "kv_pool": draw_kv_pool(jax.random.fold_in(splits[13], 71), 0),
        "prefix_len": draw_prefix_len(jax.random.fold_in(splits[13], 71), 0),
        "hit_holder": draw_hit_holder(jax.random.fold_in(splits[13], 71), 0),
        "hit_slot": set_ends(jax.random.randint(splits[10], (REQS, MAXB), 0, POOL), jax.random.fold_in(splits[10], 1), 0, POOL - 1).astype(jnp.int32),
        "dest_holder": draw_dest_holder(jax.random.fold_in(splits[13], 71), 0),
        "dest_slot": draw_dest_slot(jax.random.fold_in(splits[13], 71), 0),
    }


EPS = 1e-06
THETA = 1000000.0

def rms_scale(values, gain):
    mean_sq = lax.optimization_barrier(jnp.mean(values * values, axis=-1, keepdims=True))
    return values * lax.rsqrt(mean_sq + EPS) * gain

def rotate(values, position):
    half = values.shape[-1] // 2
    freqs = THETA ** (-2.0 * jnp.arange(half, dtype=jnp.float32) / values.shape[-1])
    angle = position[..., None] * freqs
    cosine = jnp.cos(angle)
    sine = jnp.sin(angle)
    first = values[..., :half]
    second = values[..., half:]
    return jnp.concatenate([first * cosine - second * sine, second * cosine + first * sine], axis=-1)

def reference(hidden_in, norm_gain, w_query, w_keyval, query_gain, key_gain, w_output, kv_pool, prefix_len, hit_holder, hit_slot, dest_holder, dest_slot):
    normed = rms_scale(hidden_in.astype(jnp.float32), norm_gain).astype(jnp.bfloat16)
    query = jnp.dot(normed, w_query, preferred_element_type=jnp.float32).reshape(REQS, SPAN, QH, HD)
    w_single = w_keyval.reshape(D, KVH, 2, 2 * HD)[:, :, 0].reshape(D, KVH * 2 * HD)
    keyval = jnp.dot(normed, w_single, preferred_element_type=jnp.float32).reshape(REQS, SPAN, KVH, 2, HD)
    position = (prefix_len[:, None] + jnp.arange(SPAN, dtype=jnp.int32)[None, :]).astype(jnp.float32)
    query = rotate(rms_scale(query, query_gain), position[:, :, None]).astype(jnp.bfloat16)
    new_keys = rotate(rms_scale(keyval[:, :, :, 0], key_gain), position[:, :, None]).astype(jnp.bfloat16)
    new_vals = keyval[:, :, :, 1].astype(jnp.bfloat16)
    fresh = jnp.stack([new_keys, new_vals], axis=3)
    doubled = jnp.repeat(fresh, 2, axis=2)
    rows_out = (dest_holder * POOL + dest_slot).reshape(-1).astype(jnp.int32)
    pool_after = kv_pool.at[rows_out].set(doubled.reshape(REQS * NEWB, BLK, 2 * KVH * 2 * HD))
    pool_view = kv_pool.reshape(REQS * POOL, BLK, KVH, 2, 2, HD)[:, :, :, 0]
    cached_len = MAXB * BLK

    def attend(items):
        query_row, fresh_row, length, holders, slots = items
        rows_in = (holders * POOL + slots).astype(jnp.int32)
        cached = pool_view[rows_in].reshape(cached_len, KVH, 2, HD)
        keys = jnp.concatenate([cached[:, :, 0], fresh_row[:, :, 0]], axis=0).astype(jnp.float32)
        values = jnp.concatenate([cached[:, :, 1], fresh_row[:, :, 1]], axis=0).astype(jnp.float32)
        grouped = query_row.reshape(SPAN, KVH, QH // KVH, HD).astype(jnp.float32)
        scores = jnp.einsum('cgqd,sgd->gqcs', grouped, keys) * HD ** (-0.5)
        key_pos = jnp.arange(cached_len + SPAN, dtype=jnp.int32)
        query_pos = jnp.arange(SPAN, dtype=jnp.int32)
        cached_ok = key_pos[None, :] < length
        fresh_ok = key_pos[None, :] - cached_len <= query_pos[:, None]
        visible = jnp.where(key_pos[None, :] < cached_len, cached_ok, fresh_ok)
        scores = jnp.where(visible, scores, -jnp.inf)
        top = lax.optimization_barrier(jnp.max(scores, axis=-1, keepdims=True))
        weights = jnp.exp(scores - top)
        weights = (weights / lax.optimization_barrier(jnp.sum(weights, axis=-1, keepdims=True))).astype(jnp.bfloat16)
        mixed = jnp.einsum('gqcs,sgd->cgqd', weights.astype(jnp.float32), values)
        return mixed.astype(jnp.bfloat16).reshape(SPAN, QH * HD)
    mixed = lax.map(attend, (query, fresh, prefix_len, hit_holder, hit_slot)).reshape(REQS * SPAN, QH * HD)
    width = QH * HD // N_TENSOR

    def add_group(group, total):
        left = lax.dynamic_slice_in_dim(mixed, group * width, width, 1)
        right = lax.dynamic_slice_in_dim(w_output, group * width, width, 0)
        part = jnp.dot(left, right, preferred_element_type=jnp.float32)
        rounded = lax.optimization_barrier(part.astype(jnp.bfloat16))
        return total + rounded.astype(jnp.float32)
    total = lax.fori_loop(0, N_TENSOR, add_group, jnp.zeros((REQS * SPAN, D), jnp.float32))
    return (total.astype(jnp.bfloat16), pool_after)
```

```python
import functools
import math

import jax
import jax.numpy as jnp
from jax import lax
from jax.experimental import pallas as pl
from jax.experimental.pallas import tpu as pltpu
from jax.sharding import PartitionSpec as P

EPS = 1e-06
THETA = 1000000.0
SIDE = 4
NEG = -1e30
VMEM = 58 * 2**20


def rms_scale(values, gain):
    mean_sq = jnp.mean(values * values, axis=-1, keepdims=True)
    return values * lax.rsqrt(mean_sq + EPS) * gain


def rotate(values, position):
    half = values.shape[-1] // 2
    freqs = THETA ** (-2.0 * jnp.arange(half, dtype=jnp.float32) / values.shape[-1])
    angle = position[..., None] * freqs
    cosine = jnp.cos(angle)
    sine = jnp.sin(angle)
    first = values[..., :half]
    second = values[..., half:]
    return jnp.concatenate(
        [first * cosine - second * sine, second * cosine + first * sine], axis=-1
    )


def flash(q, chunks, scale):
    rows, head = q.shape
    top = total = acc = None
    for load, mask in chunks:
        keys, vals = load()
        width = keys.shape[0]
        s = lax.dot_general(
            q, keys, (((1,), (1,)), ((), ())), preferred_element_type=jnp.float32
        )
        s = mask(s)
        part = s[:, :128]
        for k in range(1, width // 128):
            part = jnp.maximum(part, s[:, k * 128:(k + 1) * 128])
        now = jnp.max(part, axis=1, keepdims=True)
        if top is None:
            total = jnp.zeros((rows, 128), jnp.float32)
            acc = jnp.zeros((rows, head), jnp.float32)
        else:
            now = jnp.maximum(top, now)
            shrink = jnp.exp2((top - now) * scale)
            total = total * shrink
            acc = acc * shrink
        p = jnp.exp2((s - now) * scale)
        for k in range(width // 128):
            total = total + p[:, k * 128:(k + 1) * 128]
        acc = acc + jnp.dot(p.astype(jnp.bfloat16), vals, preferred_element_type=jnp.float32)
        top = now
    return top, jnp.sum(total, axis=1, keepdims=True), acc


def picked(rows_ref, info_ref, pool_ref, kv, sems, chunk):
    half = pool_ref.shape[1]
    keys = kv.shape[0]
    head = kv.shape[1] // 2
    copies = [
        pltpu.make_async_copy(pool_ref.at[rows_ref[j]], kv.at[pl.ds(j * half, half)], sems.at[j])
        for j in range(keys // half)
    ]
    for copy in copies:
        copy.start()

    def wait(part, parts):
        for copy in copies[len(copies) * part // parts:len(copies) * (part + 1) // parts]:
            copy.wait()

    def load(c):
        span = slice(c * chunk, (c + 1) * chunk)
        return kv[span, :head], kv[span, head:]

    def mask(c, s):
        if (c + 1) * chunk <= keys // 2:
            return s
        index = lax.broadcasted_iota(jnp.int32, (8, chunk), 1) + c * chunk
        pos = index // half * (2 * half) + index % half + info_ref[1] * half
        return s + jnp.where(pos < info_ref[0], 0.0, NEG)[:1]

    chunks = [
        (functools.partial(load, c), functools.partial(mask, c)) for c in range(keys // chunk)
    ]
    return wait, chunks


def heads(q_ref):
    head = q_ref.shape[1] // 2
    return jnp.concatenate([q_ref[:, :head], q_ref[:, head:]], axis=0)


def log_sums(top, total, scale):
    return top * scale + jnp.log(total) * math.log2(math.e)


def lanes_of(columns, span):
    lane = lax.broadcasted_iota(jnp.int32, (span, 128), 1)
    out = jnp.zeros((span, 128), jnp.float32)
    for k, column in enumerate(columns):
        out = jnp.where(lane == k, column, out)
    return out.T


def after_wait(wait, chunk):
    load, mask = chunk

    def waited():
        wait()
        return load()

    return waited, mask


def other_kernel(
    rows_ref, info_ref, q_hbm, pool_ref, out_ref, kv, q_ref, sems, q_sem, *, chunk
):
    span, width = q_ref.shape
    head = width // 2
    scale = head ** (-0.5) * math.log2(math.e)
    copy = pltpu.make_async_copy(q_hbm, q_ref, q_sem)
    copy.start()
    wait, chunks = picked(rows_ref, info_ref, pool_ref, kv, sems, chunk)
    copy.wait()
    q = heads(q_ref)
    for part, first in enumerate((0, len(chunks) // 2)):
        chunks[first] = after_wait(functools.partial(wait, part, 2), chunks[first])
    top, total, acc = flash(q, chunks, scale)
    out = (acc / total).astype(jnp.bfloat16)
    sums = log_sums(top, total, scale)
    columns = []
    for h in range(2):
        out_ref[:span, h * head:(h + 1) * head] = out[h * span:(h + 1) * span]
        rest = sums[h * span:(h + 1) * span]
        for _ in range(3):
            piece = rest.astype(jnp.bfloat16).astype(jnp.float32)
            columns.append(piece)
            rest = rest - piece
    stats = lanes_of(columns, span)[:16].astype(jnp.bfloat16)
    out_ref[span:span + 16] = stats[:, :width]
    out_ref[span + 16:] = stats[:, width:]


def own_kernel(
    rows_ref, info_ref, q_hbm, fresh_hbm, pool_ref, later_ref, out_ref, sum_ref,
    kv, q_ref, fresh_ref, sems, q_sem, fresh_sem, *, chunk,
):
    del later_ref
    span, width = q_ref.shape
    head = width // 2
    scale = head ** (-0.5) * math.log2(math.e)
    first = pltpu.make_async_copy(q_hbm, q_ref, q_sem)
    first.start()
    second = pltpu.make_async_copy(fresh_hbm, fresh_ref, fresh_sem)
    second.start()
    wait, chunks = picked(rows_ref, info_ref, pool_ref, kv, sems, chunk)
    first.wait()
    second.wait()

    def causal(s):
        pos = lax.broadcasted_iota(jnp.int32, s.shape, 1)
        token = lax.broadcasted_iota(jnp.int32, s.shape, 0)
        token = jnp.where(token < span, token, token - span)
        return jnp.where(pos <= token, s, NEG)

    new = (lambda: (fresh_ref[:, :head], fresh_ref[:, head:]), causal)
    chunks[0] = after_wait(functools.partial(wait, 0, 1), chunks[0])
    top, total, acc = flash(heads(q_ref), [new] + chunks, scale)
    out = acc / total
    sums = log_sums(top, total, scale)
    for h in range(2):
        out_ref[:, h * head:(h + 1) * head] = out[h * span:(h + 1) * span]
    sum_ref[...] = lanes_of([sums[:span], sums[span:]], span)[:8]


def merge_kernel(own_ref, sum_ref, other_ref, first_ref, second_ref):
    span, width = own_ref.shape
    head = width // 2
    half = span // 2
    stats = jnp.concatenate([other_ref[span:span + 16], other_ref[span + 16:]], axis=1)
    stats = stats.astype(jnp.float32)
    shares = []
    for h in range(2):
        theirs = stats[3 * h:3 * h + 1] + stats[3 * h + 1:3 * h + 2] + stats[3 * h + 2:3 * h + 3]
        gap = theirs - sum_ref[h:h + 1]
        shares += [1.0 / (1.0 + jnp.exp2(gap)), 1.0 / (1.0 + jnp.exp2(-gap))]
    row = lax.broadcasted_iota(jnp.int32, (128, span), 0)
    table = jnp.zeros((128, span), jnp.float32)
    for k, share in enumerate(shares):
        table = jnp.where(row == k, share, table)
    table = table.T
    for h in range(2):
        lanes = slice(h * head, (h + 1) * head)
        out = own_ref[:, lanes] * table[:, 2 * h:2 * h + 1]
        out = out + other_ref[:span, lanes].astype(jnp.float32) * table[:, 2 * h + 1:2 * h + 2]
        out = out.astype(jnp.bfloat16)
        first_ref[:, lanes] = out[:half]
        second_ref[:, lanes] = out[half:]


def attend(rows, info, query, query_other, fresh, pool_half, pairs):
    span, width = query.shape
    head = width // 2
    entries = rows.shape[0]
    keys = entries * pool_half.shape[1]
    vmem = pl.BlockSpec(memory_space=pltpu.VMEM)
    smem = pl.BlockSpec(memory_space=pltpu.SMEM)
    hbm = pl.BlockSpec(memory_space=pltpu.HBM)
    params = pltpu.CompilerParams(vmem_limit_bytes=VMEM)
    kv = pltpu.VMEM((keys, width), jnp.bfloat16)
    tokens = pltpu.VMEM((span, width), jnp.bfloat16)
    sems, sem = pltpu.SemaphoreType.DMA((entries,)), pltpu.SemaphoreType.DMA

    def cost(number):
        return pl.CostEstimate(
            flops=8 * span * number * head,
            bytes_accessed=2 * number * width,
            transcendentals=2 * span * number,
        )

    other = pl.pallas_call(
        functools.partial(other_kernel, chunk=512),
        out_shape=jax.ShapeDtypeStruct((span + 32, width), jnp.bfloat16),
        in_specs=[smem, smem, hbm, hbm],
        out_specs=vmem,
        scratch_shapes=[kv, tokens, sems, sem],
        compiler_params=params,
        cost_estimate=cost(keys),
        name="other",
    )(rows, info, query_other, pool_half)
    arrived = lax.ppermute(other, "tensor", pairs)
    own, sums = pl.pallas_call(
        functools.partial(own_kernel, chunk=512),
        out_shape=[
            jax.ShapeDtypeStruct((span, width), jnp.float32),
            jax.ShapeDtypeStruct((8, span), jnp.float32),
        ],
        in_specs=[smem, smem, hbm, hbm, hbm, hbm],
        out_specs=[vmem, vmem],
        scratch_shapes=[kv, tokens, tokens, sems, sem, sem],
        compiler_params=params,
        cost_estimate=cost(keys + span),
        name="own",
    )(rows, info, query, fresh, pool_half, other)
    return pl.pallas_call(
        merge_kernel,
        out_shape=[jax.ShapeDtypeStruct((span // 2, width), jnp.bfloat16)] * 2,
        in_specs=[vmem] * 3,
        out_specs=[vmem] * 2,
        compiler_params=params,
        name="merge",
    )(own, sums, arrived)


def after_kernel(*refs):
    del refs


def after(fresh, others):
    hbm = pl.BlockSpec(memory_space=pl.ANY)
    return pl.pallas_call(
        after_kernel,
        out_shape=jax.ShapeDtypeStruct(fresh.shape, fresh.dtype),
        in_specs=[hbm] * (1 + len(others)),
        out_specs=hbm,
        input_output_aliases={0: 0},
        name="after",
    )(fresh, *others)


def arrange_kernel(place_ref, w_ref, *refs):
    (stay, ahead, back), turned, sem = refs[:-2], refs[-2], refs[-1]
    columns = turned.shape[1]
    for pair in range(SIDE * SIDE // 2):
        both = w_ref[:, 2 * pair * columns:2 * (pair + 1) * columns].T
        turned[2 * pair] = both[:columns]
        turned[2 * pair + 1] = both[columns:]
    x, y = place_ref[0], place_ref[1]
    targets = [(0, j, stay, j) for j in range(SIDE)]
    targets += [(1, j, ahead, j) for j in range(SIDE)] + [(3, j, back, j) for j in range(SIDE)]
    targets += [(2, j, ahead, SIDE + j) for j in range(2)] + [(2, j, back, 2 + j) for j in range(2, SIDE)]
    copies = []
    for n, (i, j, out, slot) in enumerate(targets):
        source = turned.at[lax.rem(x + i, SIDE) * SIDE + lax.rem(y + j, SIDE)]
        copies.append(pltpu.make_async_copy(source, out.at[slot], sem.at[n]))
        copies[-1].start()
    for copy in copies:
        copy.wait()


def arrange(place, w_output):
    width, columns = w_output.shape
    columns //= SIDE * SIDE
    blocks = (SIDE, SIDE + 2, SIDE + 2)
    return pl.pallas_call(
        arrange_kernel,
        out_shape=[
            jax.ShapeDtypeStruct((n, columns, width), w_output.dtype) for n in blocks
        ],
        in_specs=[
            pl.BlockSpec(memory_space=pltpu.SMEM), pl.BlockSpec(memory_space=pltpu.VMEM)
        ],
        out_specs=[pl.BlockSpec(memory_space=pl.ANY)] * len(blocks),
        scratch_shapes=[
            pltpu.VMEM((SIDE * SIDE, columns, width), w_output.dtype),
            pltpu.SemaphoreType.DMA((SIDE * SIDE,)),
        ],
        compiler_params=pltpu.CompilerParams(vmem_limit_bytes=VMEM),
        name="arrange",
    )(place, w_output)


def project_kernel(*refs):
    mixed, (stay, ahead, back, low, high), outs = refs[:SIDE], refs[SIDE:-10], refs[-10:-6]
    m_all, w_all, sent, kept, in_sems, out_sems = refs[-6:]

    def weight(i, j):
        if i == 2:
            return low.at[j] if j < 2 else high.at[j - 2]
        return {0: stay, 1: ahead, 3: back}[i].at[j]

    arrivals = [
        pltpu.make_async_copy(mixed[i], m_all.at[i], in_sems.at[i]) for i in range(SIDE)
    ]
    order = [2, 1, 3, 0]
    for j in order:
        for i in range(SIDE):
            n = j * SIDE + i
            arrivals.append(
                pltpu.make_async_copy(weight(i, j), w_all.at[n], in_sems.at[SIDE + n])
            )
    for copy in arrivals:
        copy.start()
    for copy in arrivals[:SIDE]:
        copy.wait()
    results = []
    for step, j in enumerate(order):
        for copy in arrivals[SIDE * (step + 1):SIDE * (step + 2)]:
            copy.wait()
        total = None
        for i in range(SIDE):
            part = lax.dot_general(
                w_all[j * SIDE + i], m_all[i], (((1,), (1,)), ((), ())),
                preferred_element_type=jnp.float32,
            )
            part = part.astype(jnp.bfloat16).astype(jnp.float32)
            total = part if total is None else total + part
        result = sent.at[j - 1] if j else kept
        result[...] = total.astype(result.dtype)
        results.append(pltpu.make_async_copy(result, outs[j - 1], out_sems.at[j]))
        results[-1].start()
    for copy in results:
        copy.wait()


def project(mixed, weights):
    span, width = mixed[0].shape
    columns = weights[0].shape[1]
    hbm = pl.BlockSpec(memory_space=pltpu.HBM)
    sent = jax.ShapeDtypeStruct((columns, span), jnp.bfloat16)
    return pl.pallas_call(
        project_kernel,
        out_shape=[sent] * (SIDE - 1) + [jax.ShapeDtypeStruct((columns, span), jnp.float32)],
        in_specs=[hbm] * (SIDE + len(weights)),
        out_specs=[hbm] * SIDE,
        scratch_shapes=[
            pltpu.VMEM((SIDE, span, width), jnp.bfloat16),
            pltpu.VMEM((SIDE * SIDE, columns, width), jnp.bfloat16),
            pltpu.VMEM((SIDE - 1, columns, span), jnp.bfloat16),
            pltpu.VMEM((columns, span), jnp.float32),
            pltpu.SemaphoreType.DMA((SIDE + SIDE * SIDE,)),
            pltpu.SemaphoreType.DMA((SIDE,)),
        ],
        compiler_params=pltpu.CompilerParams(vmem_limit_bytes=VMEM),
        cost_estimate=pl.CostEstimate(
            flops=2 * span * width * columns * SIDE * SIDE,
            bytes_accessed=2 * columns * width * SIDE * SIDE,
            transcendentals=0,
        ),
        name="project",
    )(*mixed, *weights)


def store_kernel(pick_ref, have_ref, fresh_ref, pool_ref, out_ref, sems):
    rows = pool_ref.shape[0]

    def copy(s, source):
        return pltpu.make_async_copy(source, out_ref.at[s], sems.at[s])

    for s in range(rows):
        here = have_ref[s] > 0

        @pl.when(here)
        def _():
            copy(s, fresh_ref.at[pick_ref[s]]).start()

        @pl.when(jnp.logical_not(here))
        def _():
            copy(s, pool_ref.at[s]).start()

    for s in range(rows):
        copy(s, pool_ref.at[s]).wait()


def store(pick, have, gathered, kv_pool):
    smem = pl.BlockSpec(memory_space=pltpu.SMEM)
    hbm = pl.BlockSpec(memory_space=pl.ANY)
    return pl.pallas_call(
        store_kernel,
        out_shape=jax.ShapeDtypeStruct(kv_pool.shape, kv_pool.dtype),
        in_specs=[smem, smem, hbm, hbm],
        out_specs=pl.BlockSpec(memory_space=pltpu.VMEM),
        scratch_shapes=[pltpu.SemaphoreType.DMA((kv_pool.shape[0],))],
        name="store",
    )(pick, have, gathered, kv_pool)


def along_y(step):
    return [
        (x * SIDE + y, x * SIDE + (y + step) % SIDE) for x in range(SIDE) for y in range(SIDE)
    ]


def along_x(step):
    return [
        (x * SIDE + y, (x + step) % SIDE * SIDE + y) for x in range(SIDE) for y in range(SIDE)
    ]


def spread(value, along):
    return [value] + [lax.ppermute(value, "tensor", along(k)) for k in range(1, SIDE)]


def settle(subtotals, along):
    total = subtotals[-1]
    for k in range(1, SIDE):
        total = total + lax.ppermute(subtotals[k - 1], "tensor", along(k)).astype(jnp.float32)
    return total.astype(jnp.bfloat16)


def local(
    hidden_in,
    norm_gain,
    w_query,
    w_keyval,
    query_gain,
    key_gain,
    w_output,
    kv_pool,
    prefix_len,
    hit_holder,
    hit_slot,
    dest_holder,
    dest_slot,
):
    own_req = lax.axis_index("replica")
    own_group = lax.axis_index("tensor")
    x, y = own_group // SIDE, own_group % SIDE
    span = hidden_in.shape[0]
    pool_rows, block, pair_width = kv_pool.shape
    head_dim = pair_width // 2
    new_blocks = span // block

    part = own_group % 2
    pairs = [(k, k ^ 1) for k in range(SIDE * SIDE)]
    sent_half = lax.dynamic_slice_in_dim(kv_pool, part * (block // 2), block // 2, axis=1)
    pool_half = lax.all_gather(sent_half, "replica", axis=0, tiled=True)

    place = after(jnp.stack([x, y]), [sent_half])
    pieces = arrange(place, w_output)
    ahead = lax.ppermute(pieces[1], "tensor", along_x(1))
    back = lax.ppermute(pieces[2], "tensor", along_x(3))

    normed = rms_scale(hidden_in.astype(jnp.float32), norm_gain).astype(jnp.bfloat16)
    query = jnp.dot(normed, w_query, preferred_element_type=jnp.float32).reshape(span, -1, head_dim)
    length = prefix_len[own_req]
    position = (length + jnp.arange(span, dtype=jnp.int32)).astype(jnp.float32)
    query = rotate(rms_scale(query, query_gain), position[:, None]).astype(jnp.bfloat16)
    query = query.reshape(span, -1)
    projected = jnp.dot(normed, w_keyval, preferred_element_type=jnp.float32)
    new_keys = rotate(rms_scale(projected[:, :head_dim], key_gain), position).astype(jnp.bfloat16)
    new_vals = projected[:, head_dim:].astype(jnp.bfloat16)
    own_new = jnp.concatenate([new_keys, new_vals], axis=1)

    rows = hit_holder[own_req] * pool_rows + hit_slot[own_req]
    flat_holder = dest_holder.reshape(-1)
    flat_slot = dest_slot.reshape(-1)
    match = (flat_holder[None, :] == own_req) & (
        flat_slot[None, :] == jnp.arange(pool_rows)[:, None]
    )
    pick = jnp.sum(jnp.where(match, jnp.arange(flat_holder.shape[0])[None, :], 0), axis=1)
    have = jnp.any(match, axis=1).astype(jnp.int32)
    pick = pick.astype(jnp.int32)
    info = jnp.stack([length, part.astype(jnp.int32)])
    query = after(query, [ahead, back])
    far_low = lax.ppermute(ahead[SIDE:], "tensor", along_x(1))
    far_high = lax.ppermute(back[SIDE:], "tensor", along_x(3))
    query_other = lax.ppermute(query, "tensor", pairs)
    own_new = after(
        own_new, [pool_half, query, query_other, rows, info, pick, have, far_low, far_high]
    )
    gathered = lax.all_gather(
        own_new.reshape(new_blocks, block, pair_width), "replica", axis=0, tiled=True
    )
    mixed = attend(rows, info, query, query_other, own_new, pool_half, pairs)
    w_out = [pieces[0], ahead, back, far_low, far_high]
    halves = [project(spread(half, along_x), w_out) for half in mixed]
    pool_after = store(pick, have, gathered, kv_pool)
    kept = after(halves[1][-1], [pool_after])
    first = settle(halves[0], along_y)
    second = settle([*halves[1][:-1], kept], along_y)
    attended = jnp.concatenate([first, second], axis=1).T
    return (attended, pool_after)


def solution(mesh):
    return jax.shard_map(
        local,
        mesh=mesh,
        in_specs=(
            P("replica", None),
            P(),
            P(None, "tensor"),
            P(None, "tensor"),
            P(),
            P(),
            P("tensor", None),
            P("replica", None, "tensor"),
            P(),
            P(),
            P(),
            P(),
            P(),
        ),
        out_specs=(P("replica", "tensor"), P("replica", None, "tensor")),
        check_vma=False,
    )
```

```python
import functools
import math

import jax
import jax.numpy as jnp
from jax import lax
from jax.experimental import pallas as pl
from jax.experimental.pallas import tpu as pltpu
from jax.sharding import PartitionSpec as P

EPS = 1e-06
THETA = 1000000.0
SIDE = 4
NEG = -1e30
VMEM = 58 * 2**20


def rms_scale(values, gain):
    mean_sq = jnp.mean(values * values, axis=-1, keepdims=True)
    return values * lax.rsqrt(mean_sq + EPS) * gain


def rotate(values, position):
    half = values.shape[-1] // 2
    freqs = THETA ** (-2.0 * jnp.arange(half, dtype=jnp.float32) / values.shape[-1])
    angle = position[..., None] * freqs
    cosine = jnp.cos(angle)
    sine = jnp.sin(angle)
    first = values[..., :half]
    second = values[..., half:]
    return jnp.concatenate(
        [first * cosine - second * sine, second * cosine + first * sine], axis=-1
    )


def flash(q, chunks, scale):
    rows, head = q.shape
    top = total = acc = None
    for load, mask in chunks:
        keys, vals = load()
        width = keys.shape[0]
        s = lax.dot_general(
            q, keys, (((1,), (1,)), ((), ())), preferred_element_type=jnp.float32
        )
        s = mask(s)
        part = s[:, :128]
        for k in range(1, width // 128):
            part = jnp.maximum(part, s[:, k * 128:(k + 1) * 128])
        now = jnp.max(part, axis=1, keepdims=True)
        if top is None:
            total = jnp.zeros((rows, 128), jnp.float32)
            acc = jnp.zeros((rows, head), jnp.float32)
        else:
            now = jnp.maximum(top, now)
            shrink = jnp.exp2((top - now) * scale)
            total = total * shrink
            acc = acc * shrink
        p = jnp.exp2((s - now) * scale)
        for k in range(width // 128):
            total = total + p[:, k * 128:(k + 1) * 128]
        acc = acc + jnp.dot(p.astype(jnp.bfloat16), vals, preferred_element_type=jnp.float32)
        top = now
    return top, jnp.sum(total, axis=1, keepdims=True), acc


def picked(rows_ref, info_ref, pool_ref, kv, sems, chunk):
    half = pool_ref.shape[1]
    keys = kv.shape[0]
    head = kv.shape[1] // 2
    copies = [
        pltpu.make_async_copy(pool_ref.at[rows_ref[j]], kv.at[pl.ds(j * half, half)], sems.at[j])
        for j in range(keys // half)
    ]
    for copy in copies:
        copy.start()

    def wait(part, parts):
        for copy in copies[len(copies) * part // parts:len(copies) * (part + 1) // parts]:
            copy.wait()

    def load(c):
        span = slice(c * chunk, (c + 1) * chunk)
        return kv[span, :head], kv[span, head:]

    def mask(c, s):
        if (c + 1) * chunk <= keys // 2:
            return s
        index = lax.broadcasted_iota(jnp.int32, (8, chunk), 1) + c * chunk
        pos = index // half * (2 * half) + index % half + info_ref[1] * half
        return s + jnp.where(pos < info_ref[0], 0.0, NEG)[:1]

    chunks = [
        (functools.partial(load, c), functools.partial(mask, c)) for c in range(keys // chunk)
    ]
    return wait, chunks


def heads(q_ref):
    head = q_ref.shape[1] // 2
    return jnp.concatenate([q_ref[:, :head], q_ref[:, head:]], axis=0)


def log_sums(top, total, scale):
    return top * scale + jnp.log(total) * math.log2(math.e)


def lanes_of(columns, span):
    lane = lax.broadcasted_iota(jnp.int32, (span, 128), 1)
    out = jnp.zeros((span, 128), jnp.float32)
    for k, column in enumerate(columns):
        out = jnp.where(lane == k, column, out)
    return out.T


def after_wait(wait, chunk):
    load, mask = chunk

    def waited():
        wait()
        return load()

    return waited, mask


def other_kernel(
    rows_ref, info_ref, q_hbm, pool_ref, out_ref, kv, q_ref, sems, q_sem, *, chunk
):
    span, width = q_ref.shape
    head = width // 2
    scale = head ** (-0.5) * math.log2(math.e)
    copy = pltpu.make_async_copy(q_hbm, q_ref, q_sem)
    copy.start()
    wait, chunks = picked(rows_ref, info_ref, pool_ref, kv, sems, chunk)
    copy.wait()
    q = heads(q_ref)
    for part, first in enumerate((0, len(chunks) // 2)):
        chunks[first] = after_wait(functools.partial(wait, part, 2), chunks[first])
    top, total, acc = flash(q, chunks, scale)
    out = (acc / total).astype(jnp.bfloat16)
    sums = log_sums(top, total, scale)
    columns = []
    for h in range(2):
        out_ref[:span, h * head:(h + 1) * head] = out[h * span:(h + 1) * span]
        rest = sums[h * span:(h + 1) * span]
        for _ in range(3):
            piece = rest.astype(jnp.bfloat16).astype(jnp.float32)
            columns.append(piece)
            rest = rest - piece
    stats = lanes_of(columns, span)[:16].astype(jnp.bfloat16)
    out_ref[span:span + 16] = stats[:, :width]
    out_ref[span + 16:] = stats[:, width:]


def own_kernel(
    rows_ref, info_ref, q_ref, fresh_ref, pool_ref, later_ref, out_ref, sum_ref, kv, sems, *, chunk
):
    del later_ref
    span, width = q_ref.shape
    head = width // 2
    scale = head ** (-0.5) * math.log2(math.e)
    wait, chunks = picked(rows_ref, info_ref, pool_ref, kv, sems, chunk)

    def causal(s):
        pos = lax.broadcasted_iota(jnp.int32, s.shape, 1)
        token = lax.broadcasted_iota(jnp.int32, s.shape, 0)
        token = jnp.where(token < span, token, token - span)
        return jnp.where(pos <= token, s, NEG)

    new = (lambda: (fresh_ref[:, :head], fresh_ref[:, head:]), causal)
    chunks[0] = after_wait(functools.partial(wait, 0, 1), chunks[0])
    top, total, acc = flash(heads(q_ref), [new] + chunks, scale)
    out = acc / total
    sums = log_sums(top, total, scale)
    for h in range(2):
        out_ref[:, h * head:(h + 1) * head] = out[h * span:(h + 1) * span]
    sum_ref[...] = lanes_of([sums[:span], sums[span:]], span)[:8]


def merge_kernel(own_ref, sum_ref, other_ref, first_ref, second_ref):
    span, width = own_ref.shape
    head = width // 2
    half = span // 2
    stats = jnp.concatenate([other_ref[span:span + 16], other_ref[span + 16:]], axis=1)
    stats = stats.astype(jnp.float32)
    shares = []
    for h in range(2):
        theirs = stats[3 * h:3 * h + 1] + stats[3 * h + 1:3 * h + 2] + stats[3 * h + 2:3 * h + 3]
        gap = theirs - sum_ref[h:h + 1]
        shares += [1.0 / (1.0 + jnp.exp2(gap)), 1.0 / (1.0 + jnp.exp2(-gap))]
    row = lax.broadcasted_iota(jnp.int32, (128, span), 0)
    table = jnp.zeros((128, span), jnp.float32)
    for k, share in enumerate(shares):
        table = jnp.where(row == k, share, table)
    table = table.T
    for h in range(2):
        lanes = slice(h * head, (h + 1) * head)
        out = own_ref[:, lanes] * table[:, 2 * h:2 * h + 1]
        out = out + other_ref[:span, lanes].astype(jnp.float32) * table[:, 2 * h + 1:2 * h + 2]
        out = out.astype(jnp.bfloat16)
        first_ref[:, lanes] = out[:half]
        second_ref[:, lanes] = out[half:]


def attend(rows, info, query, query_other, fresh, pool_half, pairs):
    span, width = query.shape
    head = width // 2
    entries = rows.shape[0]
    keys = entries * pool_half.shape[1]
    vmem = pl.BlockSpec(memory_space=pltpu.VMEM)
    smem = pl.BlockSpec(memory_space=pltpu.SMEM)
    anywhere = pl.BlockSpec(memory_space=pl.ANY)
    params = pltpu.CompilerParams(vmem_limit_bytes=VMEM)
    kv = pltpu.VMEM((keys, width), jnp.bfloat16)
    tokens = pltpu.VMEM((span, width), jnp.bfloat16)
    sems, sem = pltpu.SemaphoreType.DMA((entries,)), pltpu.SemaphoreType.DMA

    def cost(number):
        return pl.CostEstimate(
            flops=8 * span * number * head,
            bytes_accessed=2 * number * width,
            transcendentals=2 * span * number,
        )

    other = pl.pallas_call(
        functools.partial(other_kernel, chunk=512),
        out_shape=jax.ShapeDtypeStruct((span + 32, width), jnp.bfloat16),
        in_specs=[smem, smem, anywhere, anywhere],
        out_specs=vmem,
        scratch_shapes=[kv, tokens, sems, sem],
        compiler_params=params,
        cost_estimate=cost(keys),
        name="other",
    )(rows, info, query_other, pool_half)
    arrived = lax.ppermute(other, "tensor", pairs)
    own, sums = pl.pallas_call(
        functools.partial(own_kernel, chunk=512),
        out_shape=[
            jax.ShapeDtypeStruct((span, width), jnp.float32),
            jax.ShapeDtypeStruct((8, span), jnp.float32),
        ],
        in_specs=[smem, smem, vmem, vmem, anywhere, anywhere],
        out_specs=[vmem, vmem],
        scratch_shapes=[kv, sems],
        compiler_params=params,
        cost_estimate=cost(keys + span),
        name="own",
    )(rows, info, query, fresh, pool_half, other)
    return pl.pallas_call(
        merge_kernel,
        out_shape=[jax.ShapeDtypeStruct((span // 2, width), jnp.bfloat16)] * 2,
        in_specs=[vmem] * 3,
        out_specs=[vmem] * 2,
        compiler_params=params,
        name="merge",
    )(own, sums, arrived)


def after_kernel(*refs):
    del refs


def after(fresh, others):
    hbm = pl.BlockSpec(memory_space=pl.ANY)
    return pl.pallas_call(
        after_kernel,
        out_shape=jax.ShapeDtypeStruct(fresh.shape, fresh.dtype),
        in_specs=[hbm] * (1 + len(others)),
        out_specs=hbm,
        input_output_aliases={0: 0},
        name="after",
    )(fresh, *others)


def arrange_kernel(place_ref, w_ref, *refs):
    (stay, ahead, back), turned, sem = refs[:-2], refs[-2], refs[-1]
    columns = turned.shape[1]
    for pair in range(SIDE * SIDE // 2):
        both = w_ref[:, 2 * pair * columns:2 * (pair + 1) * columns].T
        turned[2 * pair] = both[:columns]
        turned[2 * pair + 1] = both[columns:]
    x, y = place_ref[0], place_ref[1]
    targets = [(0, j, stay, j) for j in range(SIDE)]
    targets += [(1, j, ahead, j) for j in range(SIDE)] + [(3, j, back, j) for j in range(SIDE)]
    targets += [(2, j, ahead, SIDE + j) for j in range(2)] + [(2, j, back, 2 + j) for j in range(2, SIDE)]
    copies = []
    for n, (i, j, out, slot) in enumerate(targets):
        source = turned.at[lax.rem(x + i, SIDE) * SIDE + lax.rem(y + j, SIDE)]
        copies.append(pltpu.make_async_copy(source, out.at[slot], sem.at[n]))
        copies[-1].start()
    for copy in copies:
        copy.wait()


def arrange(place, w_output):
    width, columns = w_output.shape
    columns //= SIDE * SIDE
    blocks = (SIDE, SIDE + 2, SIDE + 2)
    return pl.pallas_call(
        arrange_kernel,
        out_shape=[
            jax.ShapeDtypeStruct((n, columns, width), w_output.dtype) for n in blocks
        ],
        in_specs=[
            pl.BlockSpec(memory_space=pltpu.SMEM), pl.BlockSpec(memory_space=pltpu.VMEM)
        ],
        out_specs=[pl.BlockSpec(memory_space=pl.ANY)] * len(blocks),
        scratch_shapes=[
            pltpu.VMEM((SIDE * SIDE, columns, width), w_output.dtype),
            pltpu.SemaphoreType.DMA((SIDE * SIDE,)),
        ],
        compiler_params=pltpu.CompilerParams(vmem_limit_bytes=VMEM),
        name="arrange",
    )(place, w_output)


def project_kernel(*refs):
    mixed, (stay, ahead, back, low, high), outs = refs[:SIDE], refs[SIDE:-10], refs[-10:-6]
    m_all, w_all, sent, kept, in_sems, out_sems = refs[-6:]

    def weight(i, j):
        if i == 2:
            return low.at[j] if j < 2 else high.at[j - 2]
        return {0: stay, 1: ahead, 3: back}[i].at[j]

    arrivals = [
        pltpu.make_async_copy(mixed[i], m_all.at[i], in_sems.at[i]) for i in range(SIDE)
    ]
    order = [2, 1, 3, 0]
    for j in order:
        for i in range(SIDE):
            n = j * SIDE + i
            arrivals.append(
                pltpu.make_async_copy(weight(i, j), w_all.at[n], in_sems.at[SIDE + n])
            )
    for copy in arrivals:
        copy.start()
    for copy in arrivals[:SIDE]:
        copy.wait()
    results = []
    for step, j in enumerate(order):
        for copy in arrivals[SIDE * (step + 1):SIDE * (step + 2)]:
            copy.wait()
        total = None
        for i in range(SIDE):
            part = lax.dot_general(
                w_all[j * SIDE + i], m_all[i], (((1,), (1,)), ((), ())),
                preferred_element_type=jnp.float32,
            )
            part = part.astype(jnp.bfloat16).astype(jnp.float32)
            total = part if total is None else total + part
        result = sent.at[j - 1] if j else kept
        result[...] = total.astype(result.dtype)
        results.append(pltpu.make_async_copy(result, outs[j - 1], out_sems.at[j]))
        results[-1].start()
    for copy in results:
        copy.wait()


def project(mixed, weights):
    span, width = mixed[0].shape
    columns = weights[0].shape[1]
    anywhere = pl.BlockSpec(memory_space=pl.ANY)
    sent = jax.ShapeDtypeStruct((columns, span), jnp.bfloat16)
    return pl.pallas_call(
        project_kernel,
        out_shape=[sent] * (SIDE - 1) + [jax.ShapeDtypeStruct((columns, span), jnp.float32)],
        in_specs=[anywhere] * (SIDE + len(weights)),
        out_specs=[anywhere] * SIDE,
        scratch_shapes=[
            pltpu.VMEM((SIDE, span, width), jnp.bfloat16),
            pltpu.VMEM((SIDE * SIDE, columns, width), jnp.bfloat16),
            pltpu.VMEM((SIDE - 1, columns, span), jnp.bfloat16),
            pltpu.VMEM((columns, span), jnp.float32),
            pltpu.SemaphoreType.DMA((SIDE + SIDE * SIDE,)),
            pltpu.SemaphoreType.DMA((SIDE,)),
        ],
        compiler_params=pltpu.CompilerParams(vmem_limit_bytes=VMEM),
        cost_estimate=pl.CostEstimate(
            flops=2 * span * width * columns * SIDE * SIDE,
            bytes_accessed=2 * columns * width * SIDE * SIDE,
            transcendentals=0,
        ),
        name="project",
    )(*mixed, *weights)


def store_kernel(pick_ref, have_ref, fresh_ref, pool_ref, out_ref, sems):
    rows = pool_ref.shape[0]

    def copy(s, source):
        return pltpu.make_async_copy(source, out_ref.at[s], sems.at[s])

    for s in range(rows):
        here = have_ref[s] > 0

        @pl.when(here)
        def _():
            copy(s, fresh_ref.at[pick_ref[s]]).start()

        @pl.when(jnp.logical_not(here))
        def _():
            copy(s, pool_ref.at[s]).start()

    for s in range(rows):
        copy(s, pool_ref.at[s]).wait()


def store(pick, have, gathered, kv_pool):
    smem = pl.BlockSpec(memory_space=pltpu.SMEM)
    hbm = pl.BlockSpec(memory_space=pl.ANY)
    return pl.pallas_call(
        store_kernel,
        out_shape=jax.ShapeDtypeStruct(kv_pool.shape, kv_pool.dtype),
        in_specs=[smem, smem, hbm, hbm],
        out_specs=pl.BlockSpec(memory_space=pltpu.VMEM),
        scratch_shapes=[pltpu.SemaphoreType.DMA((kv_pool.shape[0],))],
        name="store",
    )(pick, have, gathered, kv_pool)


def along_y(step):
    return [
        (x * SIDE + y, x * SIDE + (y + step) % SIDE) for x in range(SIDE) for y in range(SIDE)
    ]


def along_x(step):
    return [
        (x * SIDE + y, (x + step) % SIDE * SIDE + y) for x in range(SIDE) for y in range(SIDE)
    ]


def spread(value):
    return [value] + [lax.ppermute(value, "tensor", along_x(k)) for k in range(1, SIDE)]


def settle(subtotals, along):
    total = subtotals[-1]
    for k in (3, 1, 2):
        total = total + lax.ppermute(subtotals[k - 1], "tensor", along(k)).astype(jnp.float32)
    return total.astype(jnp.bfloat16)


def local(
    hidden_in,
    norm_gain,
    w_query,
    w_keyval,
    query_gain,
    key_gain,
    w_output,
    kv_pool,
    prefix_len,
    hit_holder,
    hit_slot,
    dest_holder,
    dest_slot,
):
    own_req = lax.axis_index("replica")
    own_group = lax.axis_index("tensor")
    x, y = own_group // SIDE, own_group % SIDE
    span = hidden_in.shape[0]
    pool_rows, block, pair_width = kv_pool.shape
    head_dim = pair_width // 2
    new_blocks = span // block

    part = own_group % 2
    pairs = [(k, k ^ 1) for k in range(SIDE * SIDE)]
    sent_half = lax.dynamic_slice_in_dim(kv_pool, part * (block // 2), block // 2, axis=1)
    pool_half = lax.all_gather(sent_half, "replica", axis=0, tiled=True)

    place = after(jnp.stack([x, y]), [sent_half])
    pieces = arrange(place, w_output)
    ahead = lax.ppermute(pieces[1], "tensor", along_x(1))
    back = lax.ppermute(pieces[2], "tensor", along_x(3))

    normed = rms_scale(hidden_in.astype(jnp.float32), norm_gain).astype(jnp.bfloat16)
    query = jnp.dot(normed, w_query, preferred_element_type=jnp.float32).reshape(span, -1, head_dim)
    length = prefix_len[own_req]
    position = (length + jnp.arange(span, dtype=jnp.int32)).astype(jnp.float32)
    query = rotate(rms_scale(query, query_gain), position[:, None]).astype(jnp.bfloat16)
    query = query.reshape(span, -1)
    projected = jnp.dot(normed, w_keyval, preferred_element_type=jnp.float32)
    new_keys = rotate(rms_scale(projected[:, :head_dim], key_gain), position).astype(jnp.bfloat16)
    new_vals = projected[:, head_dim:].astype(jnp.bfloat16)
    own_new = jnp.concatenate([new_keys, new_vals], axis=1)

    rows = hit_holder[own_req] * pool_rows + hit_slot[own_req]
    flat_holder = dest_holder.reshape(-1)
    flat_slot = dest_slot.reshape(-1)
    match = (flat_holder[None, :] == own_req) & (
        flat_slot[None, :] == jnp.arange(pool_rows)[:, None]
    )
    pick = jnp.sum(jnp.where(match, jnp.arange(flat_holder.shape[0])[None, :], 0), axis=1)
    have = jnp.any(match, axis=1).astype(jnp.int32)
    pick = pick.astype(jnp.int32)
    info = jnp.stack([length, part.astype(jnp.int32)])
    query = after(query, [ahead, back])
    far_low = lax.ppermute(ahead[SIDE:], "tensor", along_x(1))
    far_high = lax.ppermute(back[SIDE:], "tensor", along_x(3))
    query_other = lax.ppermute(query, "tensor", pairs)
    own_new = after(
        own_new, [pool_half, query, query_other, rows, info, pick, have, far_low, far_high]
    )
    gathered = lax.all_gather(
        own_new.reshape(new_blocks, block, pair_width), "replica", axis=0, tiled=True
    )
    mixed = attend(rows, info, query, query_other, own_new, pool_half, pairs)
    w_out = [pieces[0], ahead, back, far_low, far_high]
    halves = [project(spread(half), w_out) for half in mixed]
    pool_after = store(pick, have, gathered, kv_pool)
    kept = after(halves[1][-1], [pool_after])
    first = settle(halves[0], along_y)
    second = settle([*halves[1][:-1], kept], along_y)
    attended = jnp.concatenate([first, second], axis=1).T
    return (attended, pool_after)


def solution(mesh):
    return jax.shard_map(
        local,
        mesh=mesh,
        in_specs=(
            P("replica", None),
            P(),
            P(None, "tensor"),
            P(None, "tensor"),
            P(),
            P(),
            P("tensor", None),
            P("replica", None, "tensor"),
            P(),
            P(),
            P(),
            P(),
            P(),
        ),
        out_specs=(P("replica", "tensor"), P("replica", None, "tensor")),
        check_vma=False,
    )
```

```python
import functools
import math

import jax
import jax.numpy as jnp
from jax import lax
from jax.experimental import pallas as pl
from jax.experimental.pallas import tpu as pltpu
from jax.sharding import PartitionSpec as P

EPS = 1e-06
THETA = 1000000.0
SIDE = 4
NEG = -1e30
VMEM = 58 * 2**20


def rms_scale(values, gain):
    mean_sq = jnp.mean(values * values, axis=-1, keepdims=True)
    return values * lax.rsqrt(mean_sq + EPS) * gain


def rotate(values, position):
    half = values.shape[-1] // 2
    freqs = THETA ** (-2.0 * jnp.arange(half, dtype=jnp.float32) / values.shape[-1])
    angle = position[..., None] * freqs
    cosine = jnp.cos(angle)
    sine = jnp.sin(angle)
    first = values[..., :half]
    second = values[..., half:]
    return jnp.concatenate(
        [first * cosine - second * sine, second * cosine + first * sine], axis=-1
    )


def flash(q, chunks, scale):
    rows, head = q.shape
    top = total = acc = None
    for load, mask in chunks:
        keys, vals = load()
        width = keys.shape[0]
        s = lax.dot_general(
            q, keys, (((1,), (1,)), ((), ())), preferred_element_type=jnp.float32
        )
        s = mask(s)
        part = s[:, :128]
        for k in range(1, width // 128):
            part = jnp.maximum(part, s[:, k * 128:(k + 1) * 128])
        now = jnp.max(part, axis=1, keepdims=True)
        if top is None:
            total = jnp.zeros((rows, 128), jnp.float32)
            acc = jnp.zeros((rows, head), jnp.float32)
        else:
            now = jnp.maximum(top, now)
            shrink = jnp.exp2((top - now) * scale)
            total = total * shrink
            acc = acc * shrink
        p = jnp.exp2((s - now) * scale)
        for k in range(width // 128):
            total = total + p[:, k * 128:(k + 1) * 128]
        acc = acc + jnp.dot(p.astype(jnp.bfloat16), vals, preferred_element_type=jnp.float32)
        top = now
    return top, jnp.sum(total, axis=1, keepdims=True), acc


def picked(rows_ref, info_ref, pool_ref, kv, sems, chunk):
    half = pool_ref.shape[1]
    keys = kv.shape[0]
    head = kv.shape[1] // 2
    copies = [
        pltpu.make_async_copy(pool_ref.at[rows_ref[j]], kv.at[pl.ds(j * half, half)], sems.at[j])
        for j in range(keys // half)
    ]
    for copy in copies:
        copy.start()

    def wait(part, parts):
        for copy in copies[len(copies) * part // parts:len(copies) * (part + 1) // parts]:
            copy.wait()

    def load(c):
        span = slice(c * chunk, (c + 1) * chunk)
        return kv[span, :head], kv[span, head:]

    def mask(c, s):
        if (c + 1) * chunk <= keys // 2:
            return s
        index = lax.broadcasted_iota(jnp.int32, (8, chunk), 1) + c * chunk
        pos = index // half * (2 * half) + index % half + info_ref[1] * half
        return s + jnp.where(pos < info_ref[0], 0.0, NEG)[:1]

    chunks = [
        (functools.partial(load, c), functools.partial(mask, c)) for c in range(keys // chunk)
    ]
    return wait, chunks


def heads(q_ref):
    head = q_ref.shape[1] // 2
    return jnp.concatenate([q_ref[:, :head], q_ref[:, head:]], axis=0)


def log_sums(top, total, scale):
    return top * scale + jnp.log(total) * math.log2(math.e)


def lanes_of(columns, span):
    lane = lax.broadcasted_iota(jnp.int32, (span, 128), 1)
    out = jnp.zeros((span, 128), jnp.float32)
    for k, column in enumerate(columns):
        out = jnp.where(lane == k, column, out)
    return out.T


def after_wait(wait, chunk):
    load, mask = chunk

    def waited():
        wait()
        return load()

    return waited, mask


def other_kernel(
    rows_ref, info_ref, q_hbm, pool_ref, out_ref, kv, q_ref, sems, q_sem, *, chunk
):
    span, width = q_ref.shape
    head = width // 2
    scale = head ** (-0.5) * math.log2(math.e)
    copy = pltpu.make_async_copy(q_hbm, q_ref, q_sem)
    copy.start()
    wait, chunks = picked(rows_ref, info_ref, pool_ref, kv, sems, chunk)
    copy.wait()
    q = heads(q_ref)
    for part, first in enumerate((0, len(chunks) // 2)):
        chunks[first] = after_wait(functools.partial(wait, part, 2), chunks[first])
    top, total, acc = flash(q, chunks, scale)
    out = (acc / total).astype(jnp.bfloat16)
    sums = log_sums(top, total, scale)
    columns = []
    for h in range(2):
        out_ref[:span, h * head:(h + 1) * head] = out[h * span:(h + 1) * span]
        rest = sums[h * span:(h + 1) * span]
        for _ in range(3):
            piece = rest.astype(jnp.bfloat16).astype(jnp.float32)
            columns.append(piece)
            rest = rest - piece
    stats = lanes_of(columns, span)[:16].astype(jnp.bfloat16)
    out_ref[span:span + 16] = stats[:, :width]
    out_ref[span + 16:] = stats[:, width:]


def own_kernel(
    rows_ref, info_ref, q_ref, fresh_ref, pool_ref, later_ref, out_ref, sum_ref, kv, sems, *, chunk
):
    del later_ref
    span, width = q_ref.shape
    head = width // 2
    scale = head ** (-0.5) * math.log2(math.e)
    wait, chunks = picked(rows_ref, info_ref, pool_ref, kv, sems, chunk)

    def causal(s):
        pos = lax.broadcasted_iota(jnp.int32, s.shape, 1)
        token = lax.broadcasted_iota(jnp.int32, s.shape, 0)
        token = jnp.where(token < span, token, token - span)
        return jnp.where(pos <= token, s, NEG)

    new = (lambda: (fresh_ref[:, :head], fresh_ref[:, head:]), causal)
    chunks[0] = after_wait(functools.partial(wait, 0, 1), chunks[0])
    top, total, acc = flash(heads(q_ref), [new] + chunks, scale)
    out = acc / total
    sums = log_sums(top, total, scale)
    for h in range(2):
        out_ref[:, h * head:(h + 1) * head] = out[h * span:(h + 1) * span]
    sum_ref[...] = lanes_of([sums[:span], sums[span:]], span)[:8]


def merge_kernel(own_ref, sum_ref, other_ref, first_ref, second_ref):
    span, width = own_ref.shape
    head = width // 2
    half = span // 2
    stats = jnp.concatenate([other_ref[span:span + 16], other_ref[span + 16:]], axis=1)
    stats = stats.astype(jnp.float32)
    shares = []
    for h in range(2):
        theirs = stats[3 * h:3 * h + 1] + stats[3 * h + 1:3 * h + 2] + stats[3 * h + 2:3 * h + 3]
        gap = theirs - sum_ref[h:h + 1]
        shares += [1.0 / (1.0 + jnp.exp2(gap)), 1.0 / (1.0 + jnp.exp2(-gap))]
    row = lax.broadcasted_iota(jnp.int32, (128, span), 0)
    table = jnp.zeros((128, span), jnp.float32)
    for k, share in enumerate(shares):
        table = jnp.where(row == k, share, table)
    table = table.T
    for h in range(2):
        lanes = slice(h * head, (h + 1) * head)
        out = own_ref[:, lanes] * table[:, 2 * h:2 * h + 1]
        out = out + other_ref[:span, lanes].astype(jnp.float32) * table[:, 2 * h + 1:2 * h + 2]
        out = out.astype(jnp.bfloat16)
        first_ref[:, lanes] = out[:half]
        second_ref[:, lanes] = out[half:]


def attend(rows, info, query, query_other, fresh, pool_half, pairs):
    span, width = query.shape
    head = width // 2
    entries = rows.shape[0]
    keys = entries * pool_half.shape[1]
    vmem = pl.BlockSpec(memory_space=pltpu.VMEM)
    smem = pl.BlockSpec(memory_space=pltpu.SMEM)
    anywhere = pl.BlockSpec(memory_space=pl.ANY)
    params = pltpu.CompilerParams(vmem_limit_bytes=VMEM)
    kv = pltpu.VMEM((keys, width), jnp.bfloat16)
    tokens = pltpu.VMEM((span, width), jnp.bfloat16)
    sems, sem = pltpu.SemaphoreType.DMA((entries,)), pltpu.SemaphoreType.DMA

    def cost(number):
        return pl.CostEstimate(
            flops=8 * span * number * head,
            bytes_accessed=2 * number * width,
            transcendentals=2 * span * number,
        )

    other = pl.pallas_call(
        functools.partial(other_kernel, chunk=512),
        out_shape=jax.ShapeDtypeStruct((span + 32, width), jnp.bfloat16),
        in_specs=[smem, smem, anywhere, anywhere],
        out_specs=vmem,
        scratch_shapes=[kv, tokens, sems, sem],
        compiler_params=params,
        cost_estimate=cost(keys),
        name="other",
    )(rows, info, query_other, pool_half)
    arrived = in_vmem(lax.ppermute(other, "tensor", pairs))
    own, sums = pl.pallas_call(
        functools.partial(own_kernel, chunk=512),
        out_shape=[
            jax.ShapeDtypeStruct((span, width), jnp.float32),
            jax.ShapeDtypeStruct((8, span), jnp.float32),
        ],
        in_specs=[smem, smem, vmem, vmem, anywhere, anywhere],
        out_specs=[vmem, vmem],
        scratch_shapes=[kv, sems],
        compiler_params=params,
        cost_estimate=cost(keys + span),
        name="own",
    )(rows, info, query, fresh, pool_half, other)
    return pl.pallas_call(
        merge_kernel,
        out_shape=[jax.ShapeDtypeStruct((span // 2, width), jnp.bfloat16)] * 2,
        in_specs=[vmem] * 3,
        out_specs=[vmem] * 2,
        compiler_params=params,
        name="merge",
    )(own, sums, arrived)


def after_kernel(*refs):
    del refs


def after(fresh, others):
    hbm = pl.BlockSpec(memory_space=pl.ANY)
    return pl.pallas_call(
        after_kernel,
        out_shape=jax.ShapeDtypeStruct(fresh.shape, fresh.dtype),
        in_specs=[hbm] * (1 + len(others)),
        out_specs=hbm,
        input_output_aliases={0: 0},
        name="after",
    )(fresh, *others)


def arrange_kernel(place_ref, w_ref, *refs):
    (stay, ahead, back), turned, sem = refs[:-2], refs[-2], refs[-1]
    columns = turned.shape[1]
    for pair in range(SIDE * SIDE // 2):
        both = w_ref[:, 2 * pair * columns:2 * (pair + 1) * columns].T
        turned[2 * pair] = both[:columns]
        turned[2 * pair + 1] = both[columns:]
    x, y = place_ref[0], place_ref[1]
    targets = [(0, j, stay, j) for j in range(SIDE)]
    targets += [(1, j, ahead, j) for j in range(SIDE)] + [(3, j, back, j) for j in range(SIDE)]
    targets += [(2, j, ahead, SIDE + j) for j in range(2)] + [(2, j, back, 2 + j) for j in range(2, SIDE)]
    copies = []
    for n, (i, j, out, slot) in enumerate(targets):
        source = turned.at[lax.rem(x + i, SIDE) * SIDE + lax.rem(y + j, SIDE)]
        copies.append(pltpu.make_async_copy(source, out.at[slot], sem.at[n]))
        copies[-1].start()
    for copy in copies:
        copy.wait()


def arrange(place, w_output):
    width, columns = w_output.shape
    columns //= SIDE * SIDE
    blocks = (SIDE, SIDE + 2, SIDE + 2)
    return pl.pallas_call(
        arrange_kernel,
        out_shape=[
            jax.ShapeDtypeStruct((n, columns, width), w_output.dtype) for n in blocks
        ],
        in_specs=[
            pl.BlockSpec(memory_space=pltpu.SMEM), pl.BlockSpec(memory_space=pltpu.VMEM)
        ],
        out_specs=[pl.BlockSpec(memory_space=pl.ANY)] * len(blocks),
        scratch_shapes=[
            pltpu.VMEM((SIDE * SIDE, columns, width), w_output.dtype),
            pltpu.SemaphoreType.DMA((SIDE * SIDE,)),
        ],
        compiler_params=pltpu.CompilerParams(vmem_limit_bytes=VMEM),
        name="arrange",
    )(place, w_output)


def project_kernel(*refs):
    mixed, (stay, ahead, back, low, high), outs = refs[:SIDE], refs[SIDE:-9], refs[-9:-5]
    w_all, sent, kept, in_sems, out_sems = refs[-5:]

    def weight(i, j):
        if i == 2:
            return low.at[j] if j < 2 else high.at[j - 2]
        return {0: stay, 1: ahead, 3: back}[i].at[j]

    arrivals = []
    order = [2, 1, 3, 0]
    for j in order:
        for i in range(SIDE):
            n = j * SIDE + i
            arrivals.append(
                pltpu.make_async_copy(weight(i, j), w_all.at[n], in_sems.at[n])
            )
    for copy in arrivals:
        copy.start()
    results = []
    for step, j in enumerate(order):
        for copy in arrivals[SIDE * step:SIDE * (step + 1)]:
            copy.wait()
        total = None
        for i in range(SIDE):
            part = lax.dot_general(
                w_all[j * SIDE + i], mixed[i][...], (((1,), (1,)), ((), ())),
                preferred_element_type=jnp.float32,
            )
            part = part.astype(jnp.bfloat16).astype(jnp.float32)
            total = part if total is None else total + part
        result = sent.at[j - 1] if j else kept
        result[...] = total.astype(result.dtype)
        results.append(pltpu.make_async_copy(result, outs[j - 1], out_sems.at[j]))
        results[-1].start()
    for copy in results:
        copy.wait()


def project(mixed, weights):
    span, width = mixed[0].shape
    columns = weights[0].shape[1]
    anywhere = pl.BlockSpec(memory_space=pl.ANY)
    sent = jax.ShapeDtypeStruct((columns, span), jnp.bfloat16)
    return pl.pallas_call(
        project_kernel,
        out_shape=[sent] * (SIDE - 1) + [jax.ShapeDtypeStruct((columns, span), jnp.float32)],
        in_specs=[pl.BlockSpec(memory_space=pltpu.VMEM)] * SIDE + [anywhere] * len(weights),
        out_specs=[anywhere] * SIDE,
        scratch_shapes=[
            pltpu.VMEM((SIDE * SIDE, columns, width), jnp.bfloat16),
            pltpu.VMEM((SIDE - 1, columns, span), jnp.bfloat16),
            pltpu.VMEM((columns, span), jnp.float32),
            pltpu.SemaphoreType.DMA((SIDE * SIDE,)),
            pltpu.SemaphoreType.DMA((SIDE,)),
        ],
        compiler_params=pltpu.CompilerParams(vmem_limit_bytes=VMEM),
        cost_estimate=pl.CostEstimate(
            flops=2 * span * width * columns * SIDE * SIDE,
            bytes_accessed=2 * columns * width * SIDE * SIDE,
            transcendentals=0,
        ),
        name="project",
    )(*mixed, *weights)


def store_kernel(pick_ref, have_ref, fresh_ref, pool_ref, out_ref, sems):
    rows = pool_ref.shape[0]

    def copy(s, source):
        return pltpu.make_async_copy(source, out_ref.at[s], sems.at[s])

    for s in range(rows):
        here = have_ref[s] > 0

        @pl.when(here)
        def _():
            copy(s, fresh_ref.at[pick_ref[s]]).start()

        @pl.when(jnp.logical_not(here))
        def _():
            copy(s, pool_ref.at[s]).start()

    for s in range(rows):
        copy(s, pool_ref.at[s]).wait()


def store(pick, have, gathered, kv_pool):
    smem = pl.BlockSpec(memory_space=pltpu.SMEM)
    hbm = pl.BlockSpec(memory_space=pl.ANY)
    return pl.pallas_call(
        store_kernel,
        out_shape=jax.ShapeDtypeStruct(kv_pool.shape, kv_pool.dtype),
        in_specs=[smem, smem, hbm, hbm],
        out_specs=pl.BlockSpec(memory_space=pltpu.VMEM),
        scratch_shapes=[pltpu.SemaphoreType.DMA((kv_pool.shape[0],))],
        name="store",
    )(pick, have, gathered, kv_pool)


def along_y(step):
    return [
        (x * SIDE + y, x * SIDE + (y + step) % SIDE) for x in range(SIDE) for y in range(SIDE)
    ]


def along_x(step):
    return [
        (x * SIDE + y, (x + step) % SIDE * SIDE + y) for x in range(SIDE) for y in range(SIDE)
    ]


def spread(value):
    return [value] + [
        in_vmem(lax.ppermute(value, "tensor", along_x(k))) for k in range(1, SIDE)
    ]


def in_vmem(value):
    return pltpu.with_memory_space_constraint(value, pltpu.VMEM)


def settle(subtotals, along):
    total = subtotals[-1]
    for k in (3, 1, 2):
        total = total + lax.ppermute(subtotals[k - 1], "tensor", along(k)).astype(jnp.float32)
    return total.astype(jnp.bfloat16)


def local(
    hidden_in,
    norm_gain,
    w_query,
    w_keyval,
    query_gain,
    key_gain,
    w_output,
    kv_pool,
    prefix_len,
    hit_holder,
    hit_slot,
    dest_holder,
    dest_slot,
):
    own_req = lax.axis_index("replica")
    own_group = lax.axis_index("tensor")
    x, y = own_group // SIDE, own_group % SIDE
    span = hidden_in.shape[0]
    pool_rows, block, pair_width = kv_pool.shape
    head_dim = pair_width // 2
    new_blocks = span // block

    part = own_group % 2
    pairs = [(k, k ^ 1) for k in range(SIDE * SIDE)]
    sent_half = lax.dynamic_slice_in_dim(kv_pool, part * (block // 2), block // 2, axis=1)
    pool_half = lax.all_gather(sent_half, "replica", axis=0, tiled=True)

    place = after(jnp.stack([x, y]), [sent_half])
    pieces = arrange(place, w_output)
    ahead = lax.ppermute(pieces[1], "tensor", along_x(1))
    back = lax.ppermute(pieces[2], "tensor", along_x(3))

    normed = rms_scale(hidden_in.astype(jnp.float32), norm_gain).astype(jnp.bfloat16)
    query = jnp.dot(normed, w_query, preferred_element_type=jnp.float32).reshape(span, -1, head_dim)
    length = prefix_len[own_req]
    position = (length + jnp.arange(span, dtype=jnp.int32)).astype(jnp.float32)
    query = rotate(rms_scale(query, query_gain), position[:, None]).astype(jnp.bfloat16)
    query = query.reshape(span, -1)
    projected = jnp.dot(normed, w_keyval, preferred_element_type=jnp.float32)
    new_keys = rotate(rms_scale(projected[:, :head_dim], key_gain), position).astype(jnp.bfloat16)
    new_vals = projected[:, head_dim:].astype(jnp.bfloat16)
    own_new = jnp.concatenate([new_keys, new_vals], axis=1)

    rows = hit_holder[own_req] * pool_rows + hit_slot[own_req]
    flat_holder = dest_holder.reshape(-1)
    flat_slot = dest_slot.reshape(-1)
    match = (flat_holder[None, :] == own_req) & (
        flat_slot[None, :] == jnp.arange(pool_rows)[:, None]
    )
    pick = jnp.sum(jnp.where(match, jnp.arange(flat_holder.shape[0])[None, :], 0), axis=1)
    have = jnp.any(match, axis=1).astype(jnp.int32)
    pick = pick.astype(jnp.int32)
    info = jnp.stack([length, part.astype(jnp.int32)])
    query = after(query, [ahead, back])
    far_low = lax.ppermute(ahead[SIDE:], "tensor", along_x(1))
    far_high = lax.ppermute(back[SIDE:], "tensor", along_x(3))
    query_other = lax.ppermute(query, "tensor", pairs)
    own_new = after(
        own_new, [pool_half, query, query_other, rows, info, pick, have, far_low, far_high]
    )
    gathered = lax.all_gather(
        own_new.reshape(new_blocks, block, pair_width), "replica", axis=0, tiled=True
    )
    mixed = attend(rows, info, query, query_other, own_new, pool_half, pairs)
    w_out = [pieces[0], ahead, back, far_low, far_high]
    halves = [project(spread(half), w_out) for half in mixed]
    pool_after = store(pick, have, gathered, kv_pool)
    kept = after(halves[1][-1], [pool_after])
    first = settle(halves[0], along_y)
    second = settle([*halves[1][:-1], kept], along_y)
    attended = jnp.concatenate([first, second], axis=1).T
    return (attended, pool_after)


def solution(mesh):
    return jax.shard_map(
        local,
        mesh=mesh,
        in_specs=(
            P("replica", None),
            P(),
            P(None, "tensor"),
            P(None, "tensor"),
            P(),
            P(),
            P("tensor", None),
            P("replica", None, "tensor"),
            P(),
            P(),
            P(),
            P(),
            P(),
        ),
        out_specs=(P("replica", "tensor"), P("replica", None, "tensor")),
        check_vma=False,
    )
```

```python
import functools
import math

import jax
import jax.numpy as jnp
from jax import lax
from jax.experimental import pallas as pl
from jax.experimental.pallas import tpu as pltpu
from jax.sharding import PartitionSpec as P

EPS = 1e-06
THETA = 1000000.0
SIDE = 4
NEG = -1e30
VMEM = 58 * 2**20


def rms_scale(values, gain):
    mean_sq = jnp.mean(values * values, axis=-1, keepdims=True)
    return values * lax.rsqrt(mean_sq + EPS) * gain


def rotate(values, position):
    half = values.shape[-1] // 2
    freqs = THETA ** (-2.0 * jnp.arange(half, dtype=jnp.float32) / values.shape[-1])
    angle = position[..., None] * freqs
    cosine = jnp.cos(angle)
    sine = jnp.sin(angle)
    first = values[..., :half]
    second = values[..., half:]
    return jnp.concatenate(
        [first * cosine - second * sine, second * cosine + first * sine], axis=-1
    )


def flash(q, chunks, scale):
    rows, head = q.shape
    top = total = acc = None
    for load, mask in chunks:
        keys, vals = load()
        width = keys.shape[0]
        s = lax.dot_general(
            q, keys, (((1,), (1,)), ((), ())), preferred_element_type=jnp.float32
        )
        s = mask(s)
        part = s[:, :128]
        for k in range(1, width // 128):
            part = jnp.maximum(part, s[:, k * 128:(k + 1) * 128])
        now = jnp.max(part, axis=1, keepdims=True)
        if top is None:
            total = jnp.zeros((rows, 128), jnp.float32)
            acc = jnp.zeros((rows, head), jnp.float32)
        else:
            now = jnp.maximum(top, now)
            shrink = jnp.exp2((top - now) * scale)
            total = total * shrink
            acc = acc * shrink
        p = jnp.exp2((s - now) * scale)
        for k in range(width // 128):
            total = total + p[:, k * 128:(k + 1) * 128]
        acc = acc + jnp.dot(p.astype(jnp.bfloat16), vals, preferred_element_type=jnp.float32)
        top = now
    return top, jnp.sum(total, axis=1, keepdims=True), acc


def picked(rows_ref, info_ref, pool_ref, kv, sems, chunk):
    half = pool_ref.shape[1]
    keys = kv.shape[0]
    head = kv.shape[1] // 2
    copies = [
        pltpu.make_async_copy(pool_ref.at[rows_ref[j]], kv.at[pl.ds(j * half, half)], sems.at[j])
        for j in range(keys // half)
    ]
    for copy in copies:
        copy.start()

    def wait(part, parts):
        for copy in copies[len(copies) * part // parts:len(copies) * (part + 1) // parts]:
            copy.wait()

    def load(c):
        span = slice(c * chunk, (c + 1) * chunk)
        return kv[span, :head], kv[span, head:]

    def mask(c, s):
        if (c + 1) * chunk <= keys // 2:
            return s
        index = lax.broadcasted_iota(jnp.int32, (8, chunk), 1) + c * chunk
        pos = index // half * (2 * half) + index % half + info_ref[1] * half
        return s + jnp.where(pos < info_ref[0], 0.0, NEG)[:1]

    chunks = [
        (functools.partial(load, c), functools.partial(mask, c)) for c in range(keys // chunk)
    ]
    return wait, chunks


def heads(q_ref):
    head = q_ref.shape[1] // 2
    return jnp.concatenate([q_ref[:, :head], q_ref[:, head:]], axis=0)


def log_sums(top, total, scale):
    return top * scale + jnp.log(total) * math.log2(math.e)


def lanes_of(columns, span):
    lane = lax.broadcasted_iota(jnp.int32, (span, 128), 1)
    out = jnp.zeros((span, 128), jnp.float32)
    for k, column in enumerate(columns):
        out = jnp.where(lane == k, column, out)
    return out.T


def after_wait(wait, chunk):
    load, mask = chunk

    def waited():
        wait()
        return load()

    return waited, mask


def other_kernel(
    rows_ref, info_ref, q_hbm, pool_ref, out_ref, kv, q_ref, sems, q_sem, *, chunk
):
    span, width = q_ref.shape
    head = width // 2
    scale = head ** (-0.5) * math.log2(math.e)
    copy = pltpu.make_async_copy(q_hbm, q_ref, q_sem)
    copy.start()
    wait, chunks = picked(rows_ref, info_ref, pool_ref, kv, sems, chunk)
    copy.wait()
    q = heads(q_ref)
    for part, first in enumerate((0, len(chunks) // 2)):
        chunks[first] = after_wait(functools.partial(wait, part, 2), chunks[first])
    top, total, acc = flash(q, chunks, scale)
    out = (acc / total).astype(jnp.bfloat16)
    sums = log_sums(top, total, scale)
    columns = []
    for h in range(2):
        out_ref[:span, h * head:(h + 1) * head] = out[h * span:(h + 1) * span]
        rest = sums[h * span:(h + 1) * span]
        for _ in range(3):
            piece = rest.astype(jnp.bfloat16).astype(jnp.float32)
            columns.append(piece)
            rest = rest - piece
    stats = lanes_of(columns, span)[:16].astype(jnp.bfloat16)
    out_ref[span:span + 16] = stats[:, :width]
    out_ref[span + 16:] = stats[:, width:]


def own_kernel(
    rows_ref, info_ref, q_ref, fresh_ref, pool_ref, later_ref, out_ref, sum_ref, kv, sems, *, chunk
):
    del later_ref
    span, width = q_ref.shape
    head = width // 2
    scale = head ** (-0.5) * math.log2(math.e)
    wait, chunks = picked(rows_ref, info_ref, pool_ref, kv, sems, chunk)

    def causal(s):
        pos = lax.broadcasted_iota(jnp.int32, s.shape, 1)
        token = lax.broadcasted_iota(jnp.int32, s.shape, 0)
        token = jnp.where(token < span, token, token - span)
        return jnp.where(pos <= token, s, NEG)

    new = (lambda: (fresh_ref[:, :head], fresh_ref[:, head:]), causal)
    chunks[0] = after_wait(functools.partial(wait, 0, 1), chunks[0])
    top, total, acc = flash(heads(q_ref), [new] + chunks, scale)
    out = acc / total
    sums = log_sums(top, total, scale)
    for h in range(2):
        out_ref[:, h * head:(h + 1) * head] = out[h * span:(h + 1) * span]
    sum_ref[...] = lanes_of([sums[:span], sums[span:]], span)[:8]


def merge_kernel(own_ref, sum_ref, other_ref, first_ref, second_ref):
    span, width = own_ref.shape
    head = width // 2
    half = span // 2
    stats = jnp.concatenate([other_ref[span:span + 16], other_ref[span + 16:]], axis=1)
    stats = stats.astype(jnp.float32)
    shares = []
    for h in range(2):
        theirs = stats[3 * h:3 * h + 1] + stats[3 * h + 1:3 * h + 2] + stats[3 * h + 2:3 * h + 3]
        gap = theirs - sum_ref[h:h + 1]
        shares += [1.0 / (1.0 + jnp.exp2(gap)), 1.0 / (1.0 + jnp.exp2(-gap))]
    row = lax.broadcasted_iota(jnp.int32, (128, span), 0)
    table = jnp.zeros((128, span), jnp.float32)
    for k, share in enumerate(shares):
        table = jnp.where(row == k, share, table)
    table = table.T
    for h in range(2):
        lanes = slice(h * head, (h + 1) * head)
        out = own_ref[:, lanes] * table[:, 2 * h:2 * h + 1]
        out = out + other_ref[:span, lanes].astype(jnp.float32) * table[:, 2 * h + 1:2 * h + 2]
        out = out.astype(jnp.bfloat16)
        first_ref[:, lanes] = out[:half]
        second_ref[:, lanes] = out[half:]


def attend(rows, info, query, query_other, fresh, pool_half, pairs):
    span, width = query.shape
    head = width // 2
    entries = rows.shape[0]
    keys = entries * pool_half.shape[1]
    vmem = pl.BlockSpec(memory_space=pltpu.VMEM)
    smem = pl.BlockSpec(memory_space=pltpu.SMEM)
    anywhere = pl.BlockSpec(memory_space=pl.ANY)
    params = pltpu.CompilerParams(vmem_limit_bytes=VMEM)
    kv = pltpu.VMEM((keys, width), jnp.bfloat16)
    tokens = pltpu.VMEM((span, width), jnp.bfloat16)
    sems, sem = pltpu.SemaphoreType.DMA((entries,)), pltpu.SemaphoreType.DMA

    def cost(number):
        return pl.CostEstimate(
            flops=8 * span * number * head,
            bytes_accessed=2 * number * width,
            transcendentals=2 * span * number,
        )

    other = pl.pallas_call(
        functools.partial(other_kernel, chunk=512),
        out_shape=jax.ShapeDtypeStruct((span + 32, width), jnp.bfloat16),
        in_specs=[smem, smem, anywhere, anywhere],
        out_specs=vmem,
        scratch_shapes=[kv, tokens, sems, sem],
        compiler_params=params,
        cost_estimate=cost(keys),
        name="other",
    )(rows, info, query_other, pool_half)
    arrived = in_vmem(lax.ppermute(other, "tensor", pairs))
    own, sums = pl.pallas_call(
        functools.partial(own_kernel, chunk=512),
        out_shape=[
            jax.ShapeDtypeStruct((span, width), jnp.float32),
            jax.ShapeDtypeStruct((8, span), jnp.float32),
        ],
        in_specs=[smem, smem, vmem, vmem, anywhere, anywhere],
        out_specs=[vmem, vmem],
        scratch_shapes=[kv, sems],
        compiler_params=params,
        cost_estimate=cost(keys + span),
        name="own",
    )(rows, info, query, fresh, pool_half, other)
    return pl.pallas_call(
        merge_kernel,
        out_shape=[jax.ShapeDtypeStruct((span // 2, width), jnp.bfloat16)] * 2,
        in_specs=[vmem] * 3,
        out_specs=[vmem] * 2,
        compiler_params=params,
        name="merge",
    )(own, sums, arrived)


def after_kernel(*refs):
    del refs


def after(fresh, others):
    hbm = pl.BlockSpec(memory_space=pl.ANY)
    return pl.pallas_call(
        after_kernel,
        out_shape=jax.ShapeDtypeStruct(fresh.shape, fresh.dtype),
        in_specs=[hbm] * (1 + len(others)),
        out_specs=hbm,
        input_output_aliases={0: 0},
        name="after",
    )(fresh, *others)


def arrange_kernel(place_ref, w_ref, *refs):
    (stay, ahead, back), turned, sem = refs[:-2], refs[-2], refs[-1]
    columns = turned.shape[1]
    for pair in range(SIDE * SIDE // 2):
        both = w_ref[:, 2 * pair * columns:2 * (pair + 1) * columns].T
        turned[2 * pair] = both[:columns]
        turned[2 * pair + 1] = both[columns:]
    x, y = place_ref[0], place_ref[1]
    targets = [(0, j, stay, j) for j in range(SIDE)]
    targets += [(1, j, ahead, j) for j in range(SIDE)] + [(3, j, back, j) for j in range(SIDE)]
    targets += [(2, j, ahead, SIDE + j) for j in range(2)] + [(2, j, back, 2 + j) for j in range(2, SIDE)]
    copies = []
    for n, (i, j, out, slot) in enumerate(targets):
        source = turned.at[lax.rem(x + i, SIDE) * SIDE + lax.rem(y + j, SIDE)]
        copies.append(pltpu.make_async_copy(source, out.at[slot], sem.at[n]))
        copies[-1].start()
    for copy in copies:
        copy.wait()


def arrange(place, w_output):
    width, columns = w_output.shape
    columns //= SIDE * SIDE
    blocks = (SIDE, SIDE + 2, SIDE + 2)
    return pl.pallas_call(
        arrange_kernel,
        out_shape=[
            jax.ShapeDtypeStruct((n, columns, width), w_output.dtype) for n in blocks
        ],
        in_specs=[
            pl.BlockSpec(memory_space=pltpu.SMEM), pl.BlockSpec(memory_space=pltpu.VMEM)
        ],
        out_specs=[pl.BlockSpec(memory_space=pl.ANY)] * len(blocks),
        scratch_shapes=[
            pltpu.VMEM((SIDE * SIDE, columns, width), w_output.dtype),
            pltpu.SemaphoreType.DMA((SIDE * SIDE,)),
        ],
        compiler_params=pltpu.CompilerParams(vmem_limit_bytes=VMEM),
        name="arrange",
    )(place, w_output)


def project_kernel(*refs):
    mixed, (stay, ahead, back, low, high), outs = refs[:SIDE], refs[SIDE:-10], refs[-10:-6]
    here, w_all, sent, kept, in_sems, out_sems = refs[-6:]

    def weight(i, j):
        if i == 2:
            return low.at[j] if j < 2 else high.at[j - 2]
        return {0: stay, 1: ahead, 3: back}[i].at[j]

    own = pltpu.make_async_copy(mixed[0], here, in_sems.at[SIDE * SIDE])
    own.start()
    mixed = (here, *mixed[1:])
    arrivals = []
    order = [2, 1, 3, 0]
    for j in order:
        for i in range(SIDE):
            n = j * SIDE + i
            arrivals.append(
                pltpu.make_async_copy(weight(i, j), w_all.at[n], in_sems.at[n])
            )
    for copy in arrivals:
        copy.start()
    own.wait()
    results = []
    for step, j in enumerate(order):
        for copy in arrivals[SIDE * step:SIDE * (step + 1)]:
            copy.wait()
        total = None
        for i in range(SIDE):
            part = lax.dot_general(
                w_all[j * SIDE + i], mixed[i][...], (((1,), (1,)), ((), ())),
                preferred_element_type=jnp.float32,
            )
            part = part.astype(jnp.bfloat16).astype(jnp.float32)
            total = part if total is None else total + part
        result = sent.at[j - 1] if j else kept
        result[...] = total.astype(result.dtype)
        results.append(pltpu.make_async_copy(result, outs[j - 1], out_sems.at[j]))
        results[-1].start()
    for copy in results:
        copy.wait()


def project(mixed, weights):
    span, width = mixed[0].shape
    columns = weights[0].shape[1]
    anywhere = pl.BlockSpec(memory_space=pl.ANY)
    vmem = pl.BlockSpec(memory_space=pltpu.VMEM)
    sent = jax.ShapeDtypeStruct((columns, span), jnp.bfloat16)
    return pl.pallas_call(
        project_kernel,
        out_shape=[sent] * (SIDE - 1) + [jax.ShapeDtypeStruct((columns, span), jnp.float32)],
        in_specs=[anywhere] + [vmem] * (SIDE - 1) + [anywhere] * len(weights),
        out_specs=[anywhere] * SIDE,
        scratch_shapes=[
            pltpu.VMEM((span, width), jnp.bfloat16),
            pltpu.VMEM((SIDE * SIDE, columns, width), jnp.bfloat16),
            pltpu.VMEM((SIDE - 1, columns, span), jnp.bfloat16),
            pltpu.VMEM((columns, span), jnp.float32),
            pltpu.SemaphoreType.DMA((SIDE * SIDE + 1,)),
            pltpu.SemaphoreType.DMA((SIDE,)),
        ],
        compiler_params=pltpu.CompilerParams(vmem_limit_bytes=VMEM),
        cost_estimate=pl.CostEstimate(
            flops=2 * span * width * columns * SIDE * SIDE,
            bytes_accessed=2 * columns * width * SIDE * SIDE,
            transcendentals=0,
        ),
        name="project",
    )(*mixed, *weights)


def store_kernel(pick_ref, have_ref, fresh_ref, pool_ref, out_ref, sems):
    rows = pool_ref.shape[0]

    def copy(s, source):
        return pltpu.make_async_copy(source, out_ref.at[s], sems.at[s])

    for s in range(rows):
        here = have_ref[s] > 0

        @pl.when(here)
        def _():
            copy(s, fresh_ref.at[pick_ref[s]]).start()

        @pl.when(jnp.logical_not(here))
        def _():
            copy(s, pool_ref.at[s]).start()

    for s in range(rows):
        copy(s, pool_ref.at[s]).wait()


def store(pick, have, gathered, kv_pool):
    smem = pl.BlockSpec(memory_space=pltpu.SMEM)
    hbm = pl.BlockSpec(memory_space=pl.ANY)
    return pl.pallas_call(
        store_kernel,
        out_shape=jax.ShapeDtypeStruct(kv_pool.shape, kv_pool.dtype),
        in_specs=[smem, smem, hbm, hbm],
        out_specs=pl.BlockSpec(memory_space=pltpu.VMEM),
        scratch_shapes=[pltpu.SemaphoreType.DMA((kv_pool.shape[0],))],
        name="store",
    )(pick, have, gathered, kv_pool)


def along_y(step):
    return [
        (x * SIDE + y, x * SIDE + (y + step) % SIDE) for x in range(SIDE) for y in range(SIDE)
    ]


def along_x(step):
    return [
        (x * SIDE + y, (x + step) % SIDE * SIDE + y) for x in range(SIDE) for y in range(SIDE)
    ]


def spread(value):
    return [value] + [
        in_vmem(lax.ppermute(value, "tensor", along_x(k))) for k in range(1, SIDE)
    ]


def in_vmem(value):
    return pltpu.with_memory_space_constraint(value, pltpu.VMEM)


def settle(subtotals, along):
    total = subtotals[-1]
    for k in (3, 1, 2):
        total = total + lax.ppermute(subtotals[k - 1], "tensor", along(k)).astype(jnp.float32)
    return total.astype(jnp.bfloat16)


def local(
    hidden_in,
    norm_gain,
    w_query,
    w_keyval,
    query_gain,
    key_gain,
    w_output,
    kv_pool,
    prefix_len,
    hit_holder,
    hit_slot,
    dest_holder,
    dest_slot,
):
    own_req = lax.axis_index("replica")
    own_group = lax.axis_index("tensor")
    x, y = own_group // SIDE, own_group % SIDE
    span = hidden_in.shape[0]
    pool_rows, block, pair_width = kv_pool.shape
    head_dim = pair_width // 2
    new_blocks = span // block

    part = own_group % 2
    pairs = [(k, k ^ 1) for k in range(SIDE * SIDE)]
    sent_half = lax.dynamic_slice_in_dim(kv_pool, part * (block // 2), block // 2, axis=1)
    pool_half = lax.all_gather(sent_half, "replica", axis=0, tiled=True)

    place = after(jnp.stack([x, y]), [sent_half])
    pieces = arrange(place, w_output)
    ahead = lax.ppermute(pieces[1], "tensor", along_x(1))
    back = lax.ppermute(pieces[2], "tensor", along_x(3))

    normed = rms_scale(hidden_in.astype(jnp.float32), norm_gain).astype(jnp.bfloat16)
    query = jnp.dot(normed, w_query, preferred_element_type=jnp.float32).reshape(span, -1, head_dim)
    length = prefix_len[own_req]
    position = (length + jnp.arange(span, dtype=jnp.int32)).astype(jnp.float32)
    query = rotate(rms_scale(query, query_gain), position[:, None]).astype(jnp.bfloat16)
    query = query.reshape(span, -1)
    projected = jnp.dot(normed, w_keyval, preferred_element_type=jnp.float32)
    new_keys = rotate(rms_scale(projected[:, :head_dim], key_gain), position).astype(jnp.bfloat16)
    new_vals = projected[:, head_dim:].astype(jnp.bfloat16)
    own_new = jnp.concatenate([new_keys, new_vals], axis=1)

    rows = hit_holder[own_req] * pool_rows + hit_slot[own_req]
    flat_holder = dest_holder.reshape(-1)
    flat_slot = dest_slot.reshape(-1)
    match = (flat_holder[None, :] == own_req) & (
        flat_slot[None, :] == jnp.arange(pool_rows)[:, None]
    )
    pick = jnp.sum(jnp.where(match, jnp.arange(flat_holder.shape[0])[None, :], 0), axis=1)
    have = jnp.any(match, axis=1).astype(jnp.int32)
    pick = pick.astype(jnp.int32)
    info = jnp.stack([length, part.astype(jnp.int32)])
    query = after(query, [ahead, back])
    far_low = lax.ppermute(ahead[SIDE:], "tensor", along_x(1))
    far_high = lax.ppermute(back[SIDE:], "tensor", along_x(3))
    query_other = lax.ppermute(query, "tensor", pairs)
    own_new = after(
        own_new, [pool_half, query, query_other, rows, info, pick, have, far_low, far_high]
    )
    gathered = lax.all_gather(
        own_new.reshape(new_blocks, block, pair_width), "replica", axis=0, tiled=True
    )
    mixed = attend(rows, info, query, query_other, own_new, pool_half, pairs)
    w_out = [pieces[0], ahead, back, far_low, far_high]
    halves = [project(spread(half), w_out) for half in mixed]
    pool_after = store(pick, have, gathered, kv_pool)
    kept = after(halves[1][-1], [pool_after])
    first = settle(halves[0], along_y)
    second = settle([*halves[1][:-1], kept], along_y)
    attended = jnp.concatenate([first, second], axis=1).T
    return (attended, pool_after)


def solution(mesh):
    return jax.shard_map(
        local,
        mesh=mesh,
        in_specs=(
            P("replica", None),
            P(),
            P(None, "tensor"),
            P(None, "tensor"),
            P(),
            P(),
            P("tensor", None),
            P("replica", None, "tensor"),
            P(),
            P(),
            P(),
            P(),
            P(),
        ),
        out_specs=(P("replica", "tensor"), P("replica", None, "tensor")),
        check_vma=False,
    )
```

```python
import functools
import math

import jax
import jax.numpy as jnp
from jax import lax
from jax.experimental import pallas as pl
from jax.experimental.pallas import tpu as pltpu
from jax.sharding import PartitionSpec as P

EPS = 1e-06
THETA = 1000000.0
SIDE = 4
NEG = -1e30
VMEM = 58 * 2**20


def rms_scale(values, gain):
    mean_sq = jnp.mean(values * values, axis=-1, keepdims=True)
    return values * lax.rsqrt(mean_sq + EPS) * gain


def rotate(values, position):
    half = values.shape[-1] // 2
    freqs = THETA ** (-2.0 * jnp.arange(half, dtype=jnp.float32) / values.shape[-1])
    angle = position[..., None] * freqs
    cosine = jnp.cos(angle)
    sine = jnp.sin(angle)
    first = values[..., :half]
    second = values[..., half:]
    return jnp.concatenate(
        [first * cosine - second * sine, second * cosine + first * sine], axis=-1
    )


def flash(q, chunks, scale):
    rows, head = q.shape
    top = total = acc = None
    for load, mask in chunks:
        keys, vals = load()
        width = keys.shape[0]
        s = lax.dot_general(
            q, keys, (((1,), (1,)), ((), ())), preferred_element_type=jnp.float32
        )
        s = mask(s)
        part = s[:, :128]
        for k in range(1, width // 128):
            part = jnp.maximum(part, s[:, k * 128:(k + 1) * 128])
        now = jnp.max(part, axis=1, keepdims=True)
        if top is None:
            total = jnp.zeros((rows, 128), jnp.float32)
            acc = jnp.zeros((rows, head), jnp.float32)
        else:
            now = jnp.maximum(top, now)
            shrink = jnp.exp2((top - now) * scale)
            total = total * shrink
            acc = acc * shrink
        p = jnp.exp2((s - now) * scale)
        for k in range(width // 128):
            total = total + p[:, k * 128:(k + 1) * 128]
        acc = acc + jnp.dot(p.astype(jnp.bfloat16), vals, preferred_element_type=jnp.float32)
        top = now
    return top, jnp.sum(total, axis=1, keepdims=True), acc


def picked(rows_ref, info_ref, pool_ref, kv, sems, chunk):
    half = pool_ref.shape[1]
    keys = kv.shape[0]
    head = kv.shape[1] // 2
    copies = [
        pltpu.make_async_copy(pool_ref.at[rows_ref[j]], kv.at[pl.ds(j * half, half)], sems.at[j])
        for j in range(keys // half)
    ]
    for copy in copies:
        copy.start()

    def wait(part, parts):
        for copy in copies[len(copies) * part // parts:len(copies) * (part + 1) // parts]:
            copy.wait()

    def load(c):
        span = slice(c * chunk, (c + 1) * chunk)
        return kv[span, :head], kv[span, head:]

    def mask(c, s):
        if (c + 1) * chunk <= keys // 2:
            return s
        index = lax.broadcasted_iota(jnp.int32, (8, chunk), 1) + c * chunk
        pos = index // half * (2 * half) + index % half + info_ref[1] * half
        return s + jnp.where(pos < info_ref[0], 0.0, NEG)[:1]

    chunks = [
        (functools.partial(load, c), functools.partial(mask, c)) for c in range(keys // chunk)
    ]
    return wait, chunks


def heads(q_ref):
    head = q_ref.shape[1] // 2
    return jnp.concatenate([q_ref[:, :head], q_ref[:, head:]], axis=0)


def log_sums(top, total, scale):
    return top * scale + jnp.log(total) * math.log2(math.e)


def lanes_of(columns, span):
    lane = lax.broadcasted_iota(jnp.int32, (span, 128), 1)
    out = jnp.zeros((span, 128), jnp.float32)
    for k, column in enumerate(columns):
        out = jnp.where(lane == k, column, out)
    return out.T


def after_wait(wait, chunk):
    load, mask = chunk

    def waited():
        wait()
        return load()

    return waited, mask


def other_kernel(
    rows_ref, info_ref, q_hbm, pool_ref, out_ref, kv, q_ref, sems, q_sem, *, chunk
):
    span, width = q_ref.shape
    head = width // 2
    scale = head ** (-0.5) * math.log2(math.e)
    copy = pltpu.make_async_copy(q_hbm, q_ref, q_sem)
    copy.start()
    wait, chunks = picked(rows_ref, info_ref, pool_ref, kv, sems, chunk)
    copy.wait()
    q = heads(q_ref)
    for part, first in enumerate((0, len(chunks) // 2)):
        chunks[first] = after_wait(functools.partial(wait, part, 2), chunks[first])
    top, total, acc = flash(q, chunks, scale)
    out = (acc / total).astype(jnp.bfloat16)
    sums = log_sums(top, total, scale)
    columns = []
    for h in range(2):
        out_ref[:span, h * head:(h + 1) * head] = out[h * span:(h + 1) * span]
        rest = sums[h * span:(h + 1) * span]
        for _ in range(3):
            piece = rest.astype(jnp.bfloat16).astype(jnp.float32)
            columns.append(piece)
            rest = rest - piece
    stats = lanes_of(columns, span)[:16].astype(jnp.bfloat16)
    out_ref[span:span + 16] = stats[:, :width]
    out_ref[span + 16:] = stats[:, width:]


def own_kernel(
    rows_ref, info_ref, q_ref, fresh_ref, pool_ref, later_ref, out_ref, sum_ref, kv, sems, *, chunk
):
    del later_ref
    span, width = q_ref.shape
    head = width // 2
    scale = head ** (-0.5) * math.log2(math.e)
    wait, chunks = picked(rows_ref, info_ref, pool_ref, kv, sems, chunk)

    def causal(s):
        pos = lax.broadcasted_iota(jnp.int32, s.shape, 1)
        token = lax.broadcasted_iota(jnp.int32, s.shape, 0)
        token = jnp.where(token < span, token, token - span)
        return jnp.where(pos <= token, s, NEG)

    new = (lambda: (fresh_ref[:, :head], fresh_ref[:, head:]), causal)
    chunks[0] = after_wait(functools.partial(wait, 0, 1), chunks[0])
    top, total, acc = flash(heads(q_ref), [new] + chunks, scale)
    out = acc / total
    sums = log_sums(top, total, scale)
    for h in range(2):
        out_ref[:, h * head:(h + 1) * head] = out[h * span:(h + 1) * span]
    sum_ref[...] = lanes_of([sums[:span], sums[span:]], span)[:8]


def merge_kernel(own_ref, sum_ref, other_ref, first_ref, second_ref):
    span, width = own_ref.shape
    head = width // 2
    half = span // 2
    stats = jnp.concatenate([other_ref[span:span + 16], other_ref[span + 16:]], axis=1)
    stats = stats.astype(jnp.float32)
    shares = []
    for h in range(2):
        theirs = stats[3 * h:3 * h + 1] + stats[3 * h + 1:3 * h + 2] + stats[3 * h + 2:3 * h + 3]
        gap = theirs - sum_ref[h:h + 1]
        shares += [1.0 / (1.0 + jnp.exp2(gap)), 1.0 / (1.0 + jnp.exp2(-gap))]
    row = lax.broadcasted_iota(jnp.int32, (128, span), 0)
    table = jnp.zeros((128, span), jnp.float32)
    for k, share in enumerate(shares):
        table = jnp.where(row == k, share, table)
    table = table.T
    for h in range(2):
        lanes = slice(h * head, (h + 1) * head)
        out = own_ref[:, lanes] * table[:, 2 * h:2 * h + 1]
        out = out + other_ref[:span, lanes].astype(jnp.float32) * table[:, 2 * h + 1:2 * h + 2]
        out = out.astype(jnp.bfloat16)
        first_ref[:, lanes] = out[:half]
        second_ref[:, lanes] = out[half:]


def attend(rows, info, query, query_other, fresh, pool_half, pairs):
    span, width = query.shape
    head = width // 2
    entries = rows.shape[0]
    keys = entries * pool_half.shape[1]
    vmem = pl.BlockSpec(memory_space=pltpu.VMEM)
    smem = pl.BlockSpec(memory_space=pltpu.SMEM)
    anywhere = pl.BlockSpec(memory_space=pl.ANY)
    params = pltpu.CompilerParams(vmem_limit_bytes=VMEM)
    kv = pltpu.VMEM((keys, width), jnp.bfloat16)
    tokens = pltpu.VMEM((span, width), jnp.bfloat16)
    sems, sem = pltpu.SemaphoreType.DMA((entries,)), pltpu.SemaphoreType.DMA

    def cost(number):
        return pl.CostEstimate(
            flops=8 * span * number * head,
            bytes_accessed=2 * number * width,
            transcendentals=2 * span * number,
        )

    other = pl.pallas_call(
        functools.partial(other_kernel, chunk=512),
        out_shape=jax.ShapeDtypeStruct((span + 32, width), jnp.bfloat16),
        in_specs=[smem, smem, anywhere, anywhere],
        out_specs=vmem,
        scratch_shapes=[kv, tokens, sems, sem],
        compiler_params=params,
        cost_estimate=cost(keys),
        name="other",
    )(rows, info, query_other, pool_half)
    arrived = in_vmem(lax.ppermute(other, "tensor", pairs))
    own, sums = pl.pallas_call(
        functools.partial(own_kernel, chunk=512),
        out_shape=[
            pltpu.VMEM((span, width), jnp.float32),
            pltpu.VMEM((8, span), jnp.float32),
        ],
        in_specs=[smem, smem, vmem, vmem, anywhere, anywhere],
        out_specs=[vmem, vmem],
        scratch_shapes=[kv, sems],
        compiler_params=params,
        cost_estimate=cost(keys + span),
        name="own",
    )(rows, info, query, fresh, pool_half, other)
    return pl.pallas_call(
        merge_kernel,
        out_shape=[jax.ShapeDtypeStruct((span // 2, width), jnp.bfloat16)] * 2,
        in_specs=[vmem] * 3,
        out_specs=[vmem] * 2,
        compiler_params=params,
        name="merge",
    )(in_vmem(own), in_vmem(sums), arrived)


def after_kernel(*refs):
    del refs


def after(fresh, others):
    hbm = pl.BlockSpec(memory_space=pl.ANY)
    return pl.pallas_call(
        after_kernel,
        out_shape=jax.ShapeDtypeStruct(fresh.shape, fresh.dtype),
        in_specs=[hbm] * (1 + len(others)),
        out_specs=hbm,
        input_output_aliases={0: 0},
        name="after",
    )(fresh, *others)


def arrange_kernel(place_ref, w_ref, *refs):
    (stay, ahead, back), turned, sem = refs[:-2], refs[-2], refs[-1]
    columns = turned.shape[1]
    for pair in range(SIDE * SIDE // 2):
        both = w_ref[:, 2 * pair * columns:2 * (pair + 1) * columns].T
        turned[2 * pair] = both[:columns]
        turned[2 * pair + 1] = both[columns:]
    x, y = place_ref[0], place_ref[1]
    targets = [(0, j, stay, j) for j in range(SIDE)]
    targets += [(1, j, ahead, j) for j in range(SIDE)] + [(3, j, back, j) for j in range(SIDE)]
    targets += [(2, j, ahead, SIDE + j) for j in range(2)] + [(2, j, back, 2 + j) for j in range(2, SIDE)]
    copies = []
    for n, (i, j, out, slot) in enumerate(targets):
        source = turned.at[lax.rem(x + i, SIDE) * SIDE + lax.rem(y + j, SIDE)]
        copies.append(pltpu.make_async_copy(source, out.at[slot], sem.at[n]))
        copies[-1].start()
    for copy in copies:
        copy.wait()


def arrange(place, w_output):
    width, columns = w_output.shape
    columns //= SIDE * SIDE
    blocks = (SIDE, SIDE + 2, SIDE + 2)
    return pl.pallas_call(
        arrange_kernel,
        out_shape=[
            jax.ShapeDtypeStruct((n, columns, width), w_output.dtype) for n in blocks
        ],
        in_specs=[
            pl.BlockSpec(memory_space=pltpu.SMEM), pl.BlockSpec(memory_space=pltpu.VMEM)
        ],
        out_specs=[pl.BlockSpec(memory_space=pl.ANY)] * len(blocks),
        scratch_shapes=[
            pltpu.VMEM((SIDE * SIDE, columns, width), w_output.dtype),
            pltpu.SemaphoreType.DMA((SIDE * SIDE,)),
        ],
        compiler_params=pltpu.CompilerParams(vmem_limit_bytes=VMEM),
        name="arrange",
    )(place, w_output)


def project_kernel(*refs):
    mixed, (stay, ahead, back, low, high), outs = refs[:SIDE], refs[SIDE:-10], refs[-10:-6]
    here, w_all, sent, kept, in_sems, out_sems = refs[-6:]

    def weight(i, j):
        if i == 2:
            return low.at[j] if j < 2 else high.at[j - 2]
        return {0: stay, 1: ahead, 3: back}[i].at[j]

    own = pltpu.make_async_copy(mixed[0], here, in_sems.at[SIDE * SIDE])
    own.start()
    mixed = (here, *mixed[1:])
    arrivals = []
    order = [2, 1, 3, 0]
    for j in order:
        for i in range(SIDE):
            n = j * SIDE + i
            arrivals.append(
                pltpu.make_async_copy(weight(i, j), w_all.at[n], in_sems.at[n])
            )
    for copy in arrivals:
        copy.start()
    own.wait()
    results = []
    for step, j in enumerate(order):
        for copy in arrivals[SIDE * step:SIDE * (step + 1)]:
            copy.wait()
        total = None
        for i in range(SIDE):
            part = lax.dot_general(
                w_all[j * SIDE + i], mixed[i][...], (((1,), (1,)), ((), ())),
                preferred_element_type=jnp.float32,
            )
            part = part.astype(jnp.bfloat16).astype(jnp.float32)
            total = part if total is None else total + part
        result = sent.at[j - 1] if j else kept
        result[...] = total.astype(result.dtype)
        results.append(pltpu.make_async_copy(result, outs[j - 1], out_sems.at[j]))
        results[-1].start()
    for copy in results:
        copy.wait()


def project(mixed, weights):
    span, width = mixed[0].shape
    columns = weights[0].shape[1]
    anywhere = pl.BlockSpec(memory_space=pl.ANY)
    vmem = pl.BlockSpec(memory_space=pltpu.VMEM)
    sent = jax.ShapeDtypeStruct((columns, span), jnp.bfloat16)
    return pl.pallas_call(
        project_kernel,
        out_shape=[sent] * (SIDE - 1) + [jax.ShapeDtypeStruct((columns, span), jnp.float32)],
        in_specs=[anywhere] + [vmem] * (SIDE - 1) + [anywhere] * len(weights),
        out_specs=[anywhere] * SIDE,
        scratch_shapes=[
            pltpu.VMEM((span, width), jnp.bfloat16),
            pltpu.VMEM((SIDE * SIDE, columns, width), jnp.bfloat16),
            pltpu.VMEM((SIDE - 1, columns, span), jnp.bfloat16),
            pltpu.VMEM((columns, span), jnp.float32),
            pltpu.SemaphoreType.DMA((SIDE * SIDE + 1,)),
            pltpu.SemaphoreType.DMA((SIDE,)),
        ],
        compiler_params=pltpu.CompilerParams(vmem_limit_bytes=VMEM),
        cost_estimate=pl.CostEstimate(
            flops=2 * span * width * columns * SIDE * SIDE,
            bytes_accessed=2 * columns * width * SIDE * SIDE,
            transcendentals=0,
        ),
        name="project",
    )(*mixed, *weights)


def store_kernel(pick_ref, have_ref, fresh_ref, pool_ref, out_ref, sems):
    rows = pool_ref.shape[0]

    def copy(s, source):
        return pltpu.make_async_copy(source, out_ref.at[s], sems.at[s])

    for s in range(rows):
        here = have_ref[s] > 0

        @pl.when(here)
        def _():
            copy(s, fresh_ref.at[pick_ref[s]]).start()

        @pl.when(jnp.logical_not(here))
        def _():
            copy(s, pool_ref.at[s]).start()

    for s in range(rows):
        copy(s, pool_ref.at[s]).wait()


def store(pick, have, gathered, kv_pool):
    smem = pl.BlockSpec(memory_space=pltpu.SMEM)
    hbm = pl.BlockSpec(memory_space=pl.ANY)
    return pl.pallas_call(
        store_kernel,
        out_shape=jax.ShapeDtypeStruct(kv_pool.shape, kv_pool.dtype),
        in_specs=[smem, smem, hbm, hbm],
        out_specs=pl.BlockSpec(memory_space=pltpu.VMEM),
        scratch_shapes=[pltpu.SemaphoreType.DMA((kv_pool.shape[0],))],
        name="store",
    )(pick, have, gathered, kv_pool)


def along_y(step):
    return [
        (x * SIDE + y, x * SIDE + (y + step) % SIDE) for x in range(SIDE) for y in range(SIDE)
    ]


def along_x(step):
    return [
        (x * SIDE + y, (x + step) % SIDE * SIDE + y) for x in range(SIDE) for y in range(SIDE)
    ]


def spread(value):
    return [value] + [
        in_vmem(lax.ppermute(value, "tensor", along_x(k))) for k in range(1, SIDE)
    ]


def in_vmem(value):
    return pltpu.with_memory_space_constraint(value, pltpu.VMEM)


def settle(subtotals, along):
    total = subtotals[-1]
    for k in (3, 1, 2):
        total = total + lax.ppermute(subtotals[k - 1], "tensor", along(k)).astype(jnp.float32)
    return total.astype(jnp.bfloat16)


def local(
    hidden_in,
    norm_gain,
    w_query,
    w_keyval,
    query_gain,
    key_gain,
    w_output,
    kv_pool,
    prefix_len,
    hit_holder,
    hit_slot,
    dest_holder,
    dest_slot,
):
    own_req = lax.axis_index("replica")
    own_group = lax.axis_index("tensor")
    x, y = own_group // SIDE, own_group % SIDE
    span = hidden_in.shape[0]
    pool_rows, block, pair_width = kv_pool.shape
    head_dim = pair_width // 2
    new_blocks = span // block

    part = own_group % 2
    pairs = [(k, k ^ 1) for k in range(SIDE * SIDE)]
    sent_half = lax.dynamic_slice_in_dim(kv_pool, part * (block // 2), block // 2, axis=1)
    pool_half = lax.all_gather(sent_half, "replica", axis=0, tiled=True)

    place = after(jnp.stack([x, y]), [sent_half])
    pieces = arrange(place, w_output)
    ahead = lax.ppermute(pieces[1], "tensor", along_x(1))
    back = lax.ppermute(pieces[2], "tensor", along_x(3))

    normed = rms_scale(hidden_in.astype(jnp.float32), norm_gain).astype(jnp.bfloat16)
    query = jnp.dot(normed, w_query, preferred_element_type=jnp.float32).reshape(span, -1, head_dim)
    length = prefix_len[own_req]
    position = (length + jnp.arange(span, dtype=jnp.int32)).astype(jnp.float32)
    query = rotate(rms_scale(query, query_gain), position[:, None]).astype(jnp.bfloat16)
    query = query.reshape(span, -1)
    projected = jnp.dot(normed, w_keyval, preferred_element_type=jnp.float32)
    new_keys = rotate(rms_scale(projected[:, :head_dim], key_gain), position).astype(jnp.bfloat16)
    new_vals = projected[:, head_dim:].astype(jnp.bfloat16)
    own_new = jnp.concatenate([new_keys, new_vals], axis=1)

    rows = hit_holder[own_req] * pool_rows + hit_slot[own_req]
    flat_holder = dest_holder.reshape(-1)
    flat_slot = dest_slot.reshape(-1)
    match = (flat_holder[None, :] == own_req) & (
        flat_slot[None, :] == jnp.arange(pool_rows)[:, None]
    )
    pick = jnp.sum(jnp.where(match, jnp.arange(flat_holder.shape[0])[None, :], 0), axis=1)
    have = jnp.any(match, axis=1).astype(jnp.int32)
    pick = pick.astype(jnp.int32)
    info = jnp.stack([length, part.astype(jnp.int32)])
    query = after(query, [ahead, back])
    far_low = lax.ppermute(ahead[SIDE:], "tensor", along_x(1))
    far_high = lax.ppermute(back[SIDE:], "tensor", along_x(3))
    query_other = lax.ppermute(query, "tensor", pairs)
    own_new = after(
        own_new, [pool_half, query, query_other, rows, info, pick, have, far_low, far_high]
    )
    gathered = lax.all_gather(
        own_new.reshape(new_blocks, block, pair_width), "replica", axis=0, tiled=True
    )
    mixed = attend(rows, info, query, query_other, own_new, pool_half, pairs)
    w_out = [pieces[0], ahead, back, far_low, far_high]
    halves = [project(spread(half), w_out) for half in mixed]
    pool_after = store(pick, have, gathered, kv_pool)
    kept = after(halves[1][-1], [pool_after])
    first = settle(halves[0], along_y)
    second = settle([*halves[1][:-1], kept], along_y)
    attended = jnp.concatenate([first, second], axis=1).T
    return (attended, pool_after)


def solution(mesh):
    return jax.shard_map(
        local,
        mesh=mesh,
        in_specs=(
            P("replica", None),
            P(),
            P(None, "tensor"),
            P(None, "tensor"),
            P(),
            P(),
            P("tensor", None),
            P("replica", None, "tensor"),
            P(),
            P(),
            P(),
            P(),
            P(),
        ),
        out_specs=(P("replica", "tensor"), P("replica", None, "tensor")),
        check_vma=False,
    )
```
